512 devices in a mesh: dp: 32 (over y_hi, z), item: 16 (over x, y_lo, core).
Axes of the slice: x: 4, y: 8 (y_hi: 4, y_lo: 2; y = y_hi * 2 + y_lo), z: 8, core: 2. Of those that a mesh axis runs over, the one named last changes fastest.
Arguments:
- states: bfloat16 [262144, 256], P(('dp', 'item')), may hold values from -6 to 6
- next_states: bfloat16 [262144, 256], P(('dp', 'item')), may hold values from -6 to 6
- rewards: float32 [262144], P(('dp', 'item')), may hold values from 0 to 2
- slate_ids: int32 [262144, 10], P(('dp', 'item')), may hold values from 0 to 4095
- chosen: int32 [262144], P(('dp', 'item')), may hold values from 0 to 9
- next_slate: int32 [262144, 10], P(('dp', 'item')), may hold values from 0 to 4095
- table: float32 [16384, 128], P('item'), may hold values from -100 to 100
- first_moment: float32 [16384, 128], P('item'), may hold values from -0.15625 to 0.15625
- second_moment: float32 [16384, 128], P('item'), may hold values from 1e-06 to 0.0001
- cand_rows: int32 [4096], P('item'), may hold values from 0 to 1023, as said below
- w_hidden: bfloat16 [256, 512], replicated, may hold values from -0.375 to 0.375
- w_embed: bfloat16 [512, 128], replicated, may hold values from -0.25 to 0.25
Outputs:
- new_first: float32 [16384, 128], P('item')
- new_second: float32 [16384, 128], P('item')
- direction: float32 [16384, 128], P('item')
- grad_hidden: float32 [256, 512], replicated
- grad_embed: float32 [512, 128], replicated
- td_error: float32 [262144], P(('dp', 'item'))
The draws below stay inside these ranges and needn't reach their ends.
Inputs may be any that keep to these rules, and one draw needn't show every extreme that they name: `cand_rows`: within each aligned block of 256 entries the entries are distinct.
All inputs are finite; a program needn't handle non-finite values.
Results may differ from the reference program's by a relative error of at most 0.006.
Values may be sent and summed in bfloat16 or wider, within the bound.
No kernel may reach another device: no remote copies, remote signals or barrier semaphores. Data moves between devices by JAX's collectives and lax.ppermute only.
A program may use at most 64 MiB of HBM per device.

```python
import math
import jax
import jax.numpy as jnp
from jax import lax

E = 128
F = 256
H = 512
SLATE = 10
ADAM_STEP = 10
B_DEV = 512
CAND_DEV = 256
ITEM_DEV = 1024
CANDS = 4096
ITEMS = 16384
SESS = 262144


def draw_table(key, part):
    key = jax.random.fold_in(key, 11)
    first = jax.random.fold_in(key, 0)
    values = jax.random.normal(first, (ITEMS, E), jnp.float32) * 0.35
    return values


def draw_cand_rows(key, part):
    key = jax.random.fold_in(key, 23)
    blocks = CANDS // CAND_DEV

    def one_block(block_key):
        left, right = jax.random.split(block_key)
        inner = jax.random.permutation(left, ITEM_DEV - 2)[:CAND_DEV - 2] + 1
        rows = jnp.concatenate([inner.astype(jnp.int32), jnp.array([0, ITEM_DEV - 1], jnp.int32)])
        order = jax.random.permutation(right, CAND_DEV)
        return rows[order]
    keys = jax.random.split(key, blocks)
    return jax.vmap(one_block)(keys).reshape(CANDS).astype(jnp.int32)


def plant(drawn, key, least, top_value):
    longest = drawn.shape.index(max(drawn.shape))
    spots = []
    for shift in (0, 1):
        where = [jax.random.randint(jax.random.fold_in(key, axis), (), 0, length) for axis, length in enumerate(drawn.shape)]
        where[longest] = (where[longest] + shift) % drawn.shape[longest]
        spots.append(tuple(where))
    return drawn.at[spots[0]].set(least).at[spots[1]].set(top_value)


def levels(own_key, shape, cuts, least, top_value):
    gain = 1.0
    for axis_at, shards_of in cuts:
        steps = jax.random.uniform(jax.random.fold_in(jax.random.fold_in(own_key, 6), axis_at), (shards_of,), jnp.float32, least / len(cuts), top_value / len(cuts))
        gain = gain * jnp.repeat(jnp.exp(steps), shape[axis_at] // shards_of).reshape((-1,) + (1,) * (len(shape) - 1 - axis_at))
    return gain


def scatter_about(rng, dims, deviation, reach, shards=(), kind=jnp.bfloat16):
    loudness = levels(rng, dims, shards, -0.22, 0.18) if shards else 1.0
    drawn = jax.random.normal(rng, dims, jnp.float32) * deviation * loudness
    return jnp.minimum(jnp.maximum(drawn, -reach), reach).astype(kind)


def setup_inputs(seed: int = 0) -> dict:
    key_list = jax.random.split(jax.random.key(seed), 13)
    states = scatter_about(key_list[0], (SESS, F), 1.0, 6.0, ((0, 512),))
    next_states = scatter_about(key_list[1], (SESS, F), 1.0, 6.0, ((0, 512),))
    rewards = jnp.clip(2.0 * jax.random.uniform(key_list[2], (SESS,), jnp.float32) ** levels(key_list[2], (SESS,), ((0, 512),), -0.2, 0.2), 0.0, 2.0)
    slate_ids = plant(jax.random.randint(key_list[3], (SESS, SLATE), 0, CANDS), jax.random.fold_in(key_list[3], 1), 0, CANDS - 1).astype(jnp.int32)
    chosen = plant(jax.random.randint(key_list[4], (SESS,), 0, SLATE), jax.random.fold_in(key_list[4], 1), 0, SLATE - 1).astype(jnp.int32)
    next_slate = plant(jax.random.randint(key_list[5], (SESS, SLATE), 0, CANDS), jax.random.fold_in(key_list[5], 1), 0, CANDS - 1).astype(jnp.int32)
    table = draw_table(jax.random.fold_in(key_list[12], 71), 0)
    first_moment = scatter_about(key_list[7], (ITEMS, E), 0.01, 0.15625, ((0, 16),), jnp.float32)
    second_moment = jnp.clip(jnp.exp(math.log(0.0001) - 4.6051702 * jax.random.uniform(key_list[8], (ITEMS, E), jnp.float32) ** levels(key_list[8], (ITEMS, E), ((0, 16),), -0.2, 0.2)), 9.999999974752427e-07, 0.0001)
    cand_rows = draw_cand_rows(jax.random.fold_in(key_list[12], 71), 0)
    w_hidden = scatter_about(key_list[10], (F, H), F ** -0.5, 0.375)
    w_embed = scatter_about(key_list[11], (H, E), H ** -0.5, 0.25)
    return {"states": states, "next_states": next_states, "rewards": rewards, "slate_ids": slate_ids, "chosen": chosen, "next_slate": next_slate, "table": table, "first_moment": first_moment, "second_moment": second_moment, "cand_rows": cand_rows, "w_hidden": w_hidden, "w_embed": w_embed}


PENALTY = 0.5
DISCOUNT = 0.9
BETA_ONE = 0.9
BETA_TWO = 0.999
EPSILON = 1e-08

def tower(features, w_hidden, w_embed):
    hidden = jnp.maximum(jnp.dot(features, w_hidden, preferred_element_type=jnp.float32), 0.0).astype(jnp.bfloat16)
    users = jnp.dot(hidden, w_embed, preferred_element_type=jnp.float32).astype(jnp.bfloat16)
    return (hidden, users)

def reference(states, next_states, rewards, slate_ids, chosen, next_slate, table, first_moment, second_moment, cand_rows, w_hidden, w_embed):
    owner_row = jnp.arange(CANDS, dtype=jnp.int32) // CAND_DEV * ITEM_DEV + cand_rows.astype(jnp.int32)
    slab = table[owner_row].astype(jnp.bfloat16)
    nblocks = SESS // B_DEV
    cand_index = jnp.arange(CANDS, dtype=jnp.int32)

    def block(carry, inputs):
        cand_grad, grad_hid, grad_emb = carry
        feats, next_feats, reward, slate, picked, upcoming = inputs
        hidden, users = tower(feats, w_hidden, w_embed)
        _, next_users = tower(next_feats, w_hidden, w_embed)
        scores = jnp.dot(users, slab.T, preferred_element_type=jnp.float32)
        highest = lax.optimization_barrier(jnp.max(scores, axis=1, keepdims=True))
        lse = highest[:, 0] + jnp.log(lax.optimization_barrier(jnp.sum(jnp.exp(scores - highest), axis=1)))
        slate_q = jnp.einsum('bse,be->bs', slab[slate].astype(jnp.float32), users.astype(jnp.float32))
        next_q = jnp.einsum('bse,be->bs', slab[upcoming].astype(jnp.float32), next_users.astype(jnp.float32))
        weights = jax.nn.softmax(next_q, axis=1)
        target = reward + DISCOUNT * lax.optimization_barrier(jnp.sum(weights * next_q, axis=1))
        picked_q = jnp.take_along_axis(slate_q, picked[:, None], axis=1)[:, 0]
        delta = picked_q - target
        clicked = jnp.take_along_axis(slate, picked[:, None], axis=1)[:, 0]
        onehot = (clicked[:, None] == cand_index[None, :]).astype(jnp.float32)
        score_grad = ((PENALTY * jnp.exp(scores - lse[:, None]) + (delta - PENALTY)[:, None] * onehot) / B_DEV).astype(jnp.bfloat16)
        user_grad = jnp.dot(score_grad, slab, preferred_element_type=jnp.float32).astype(jnp.bfloat16)
        cand_grad = cand_grad + jnp.dot(score_grad.T, users, preferred_element_type=jnp.float32)
        grad_emb = grad_emb + jnp.dot(hidden.T, user_grad, preferred_element_type=jnp.float32)
        back = jnp.dot(user_grad, w_embed.T, preferred_element_type=jnp.float32)
        pre_grad = jnp.where(hidden > 0, back, 0.0).astype(jnp.bfloat16)
        grad_hid = grad_hid + jnp.dot(feats.T, pre_grad, preferred_element_type=jnp.float32)
        return ((cand_grad, grad_hid, grad_emb), delta)
    inputs = (states.reshape(nblocks, B_DEV, F), next_states.reshape(nblocks, B_DEV, F), rewards.reshape(nblocks, B_DEV), slate_ids.reshape(nblocks, B_DEV, SLATE), chosen.reshape(nblocks, B_DEV), next_slate.reshape(nblocks, B_DEV, SLATE))
    start = (jnp.zeros((CANDS, E), jnp.float32), jnp.zeros((F, H), jnp.float32), jnp.zeros((H, E), jnp.float32))
    (cand_grad, grad_hidden, grad_embed), deltas = lax.scan(block, start, inputs)
    table_grad = jnp.zeros((ITEMS, E), jnp.float32).at[owner_row].add(cand_grad)
    new_first = BETA_ONE * first_moment + (1.0 - BETA_ONE) * table_grad
    new_second = BETA_TWO * second_moment + (1.0 - BETA_TWO) * table_grad * table_grad
    correct_one = 1.0 - BETA_ONE ** ADAM_STEP
    correct_two = 1.0 - BETA_TWO ** ADAM_STEP
    direction = new_first / correct_one / (jnp.sqrt(new_second / correct_two) + EPSILON)
    return (new_first, new_second, direction, grad_hidden, grad_embed, deltas.reshape(SESS))
```

```python
import jax
import jax.numpy as jnp
from jax import lax
from jax.experimental import pallas as pl
from jax.experimental.pallas import tpu as pltpu
from jax.sharding import Mesh
from jax.sharding import PartitionSpec as P

ADAM_STEP = 10
PENALTY = 0.5
DISCOUNT = 0.9
BETA_ONE = 0.9
BETA_TWO = 0.999
EPSILON = 1e-08

AXES = ("h", "z", "x", "l", "c")
SIZES = (4, 8, 4, 2, 2)
ITEM = ("x", "l", "c")
CHIPS = 8
CORES = 2
BLOCK = 256
PACK = 352
SLATE = 10
F32 = jnp.float32
BF16 = jnp.bfloat16
NT = (((1,), (1,)), ((), ()))
NN = (((1,), (0,)), ((), ()))
PARAMS = pltpu.CompilerParams(vmem_limit_bytes=48 * 1024 * 1024)


def dot(left, right, dims=NN):
    return lax.dot_general(left, right, dims, preferred_element_type=F32)


def gather_kernel(rows_ref, table_ref, out_ref):
    row = rows_ref[...].astype(F32)
    eye = lax.broadcasted_iota(jnp.int32, (128, 128), 0) == lax.broadcasted_iota(
        jnp.int32, (128, 128), 1
    )
    width = table_ref.shape[0]
    lane = lax.broadcasted_iota(jnp.int32, (128, width), 1).astype(F32)
    table = table_ref[...].astype(BF16)
    for half in range(BLOCK // 128):
        part = row[:, half * 128 : half * 128 + 128]
        column = jnp.sum(jnp.where(eye, part, 0.0), axis=1, keepdims=True)
        onehot = (lane == column).astype(F32).astype(BF16)
        slab = dot(onehot, table).astype(BF16)
        for copy in range(out_ref.shape[0]):
            out_ref[copy, half * 128 : half * 128 + 128, :] = slab


def main_kernel(
    core_ref,
    states_ref,
    next_ref,
    rewards_ref,
    slate_ref,
    chosen_ref,
    upcoming_ref,
    own_ref,
    other_ref,
    w_hidden_ref,
    w_embed_ref,
    keep_ref,
    send_ref,
    delta_ref,
    hidden_t_ref,
    users_t_ref,
    next_users_ref,
    scores_ref,
    next_scores_ref,
    low_ref,
    high_ref,
    next_q_ref,
    grad_ref,
    grad_hidden_ref,
    grad_embed_ref,
):
    core = core_ref[0]
    sessions = states_ref.shape[0]
    slabs = (own_ref, other_ref)
    outs = (keep_ref, send_ref)
    w_hidden = w_hidden_ref[...]
    w_embed = w_embed_ref[...]

    hidden_t = jnp.maximum(dot(w_hidden.T, states_ref[...], NT), 0.0).astype(BF16)
    hidden_t_ref[...] = hidden_t
    users_t_ref[...] = dot(w_embed.T, hidden_t).astype(BF16)
    next_hidden = jnp.maximum(dot(next_ref[...], w_hidden), 0.0).astype(BF16)
    next_users_ref[...] = dot(next_hidden, w_embed).astype(BF16)

    flip = core * BLOCK
    slate = jnp.bitwise_xor(slate_ref[...], flip)
    place = lax.broadcasted_iota(jnp.int32, slate.shape, 0)
    clicked = jnp.sum(jnp.where(place == chosen_ref[...], slate, 0), axis=0, keepdims=True)
    upcoming = jnp.bitwise_xor(upcoming_ref[...], flip)
    padded = jnp.concatenate(
        [upcoming, jnp.zeros((128 - SLATE, sessions), jnp.int32)], axis=0
    )
    for part in range(sessions // 128):
        rows = slice(part * 128, part * 128 + 128)
        turned = padded[:, rows].astype(F32).T.astype(jnp.int32)
        low_ref[rows, :] = jnp.bitwise_and(turned, 127)
        high_ref[rows, :] = lax.shift_right_logical(turned, 7)

    sub = lax.broadcasted_iota(jnp.int32, (8, sessions), 0)
    behind = jnp.broadcast_to(clicked, (8, sessions)) - sub

    def forward(chip, carry):
        highest, picked = carry
        for side in range(CORES):
            block = chip * CORES + side
            slab = slabs[side][chip]
            scores = dot(slab, users_t_ref[...])
            scores_ref[block] = scores
            first = block * BLOCK
            for step in range(BLOCK // 8):
                piece = scores[step * 8 : step * 8 + 8]
                highest = jnp.maximum(highest, piece)
                picked = picked + jnp.where(behind == first + step * 8, piece, 0.0)
            next_scores = dot(next_users_ref[...], slab, NT)
            next_scores_ref[block * 2] = next_scores[:, :128]
            next_scores_ref[block * 2 + 1] = next_scores[:, 128:]
        return highest, picked

    highest, picked = lax.fori_loop(
        0,
        CHIPS,
        forward,
        (jnp.full((8, sessions), -jnp.inf, F32), jnp.zeros((8, sessions), F32)),
    )
    highest = jnp.max(highest, axis=0, keepdims=True)
    picked = jnp.sum(picked, axis=0, keepdims=True)

    def look_up(group, _):
        for inner in range(2):
            rows = pl.ds(pl.multiple_of(group * 16 + inner * 8, 8), 8)
            low = low_ref[rows, :]
            high = high_ref[rows, :]
            found = jnp.zeros((8, 128), F32)
            for chunk in range(next_scores_ref.shape[0]):
                piece = jnp.take_along_axis(next_scores_ref[chunk, rows, :], low, axis=1)
                found = jnp.where(high == chunk, piece, found)
            next_q_ref[rows, :] = found
        return 0

    lax.fori_loop(0, sessions // 16, look_up, 0)
    next_q = jnp.concatenate(
        [next_q_ref[part * 128 : part * 128 + 128, :].T[:16] for part in range(sessions // 128)],
        axis=1,
    )
    shown = lax.broadcasted_iota(jnp.int32, next_q.shape, 0) < SLATE
    top = jnp.max(jnp.where(shown, next_q, -jnp.inf), axis=0, keepdims=True)
    weights = jnp.where(shown, jnp.exp(next_q - top), 0.0)
    mean = jnp.sum(jnp.where(shown, weights * next_q, 0.0), axis=0, keepdims=True) / jnp.sum(
        weights, axis=0, keepdims=True
    )
    delta = picked - (rewards_ref[...] + DISCOUNT * mean)
    delta_ref[...] = delta

    def exponentials(block, total):
        for step in range(BLOCK // 8):
            rows = slice(step * 8, step * 8 + 8)
            piece = jnp.exp(scores_ref[block, rows, :] - highest)
            scores_ref[block, rows, :] = piece
            total = total + piece
        return total

    total = lax.fori_loop(
        0, CHIPS * CORES, exponentials, jnp.zeros((8, sessions), F32)
    )
    total = jnp.sum(total, axis=0, keepdims=True)
    scale = 1.0 / sessions
    gain = jnp.broadcast_to((PENALTY * scale) / total, (8, sessions))
    extra = jnp.broadcast_to((delta - PENALTY) * scale, (8, sessions))

    def backward(chip, user_grad_t):
        for side in range(CORES):
            block = chip * CORES + side
            first = block * BLOCK
            for step in range(BLOCK // 16):
                pieces = []
                for inner in range(2):
                    row = step * 16 + inner * 8
                    piece = scores_ref[block, row : row + 8, :] * gain
                    pieces.append(piece + jnp.where(behind == first + row, extra, 0.0))
                grad_ref[step * 16 : step * 16 + 16, :] = jnp.concatenate(pieces, axis=0).astype(
                    BF16
                )
            grad = grad_ref[...]
            slab = slabs[side][chip]
            user_grad_t = user_grad_t + dot(slab.T, grad)
            outs[side][chip, :BLOCK, :] = dot(grad, users_t_ref[...], NT).astype(BF16)
        return user_grad_t

    embed = own_ref.shape[2]
    user_grad_t = lax.fori_loop(0, CHIPS, backward, jnp.zeros((embed, sessions), F32)).astype(BF16)

    hidden_t = hidden_t_ref[...]
    grad_embed_ref[...] = dot(hidden_t, user_grad_t, NT)
    back = dot(w_embed, user_grad_t)
    pre_grad_t = jnp.where(hidden_t.astype(F32) > 0, back, 0.0).astype(BF16)
    grad_hidden_ref[...] = dot(states_ref[...].T, pre_grad_t, NT)
    for chip in range(CHIPS):
        for side in range(CORES):
            index = chip * CORES + jnp.bitwise_xor(core, side)
            rows = pl.ds(pl.multiple_of(index * 16, 16), 16)
            for quarter in range(4):
                at = BLOCK + quarter * 16
                outs[side][chip, at : at + 16, :] = grad_hidden_ref[
                    rows, quarter * 128 : quarter * 128 + 128
                ].astype(BF16)
            rows = pl.ds(pl.multiple_of(index * 32, 32), 32)
            outs[side][chip, BLOCK + 64 :, :] = grad_embed_ref[rows, :].astype(BF16)


def adam_kernel(
    rows_ref, grad_ref, first_ref, second_ref, tower_ref, new_first_ref, new_second_ref,
    direction_ref, grad_hidden_ref, grad_embed_ref,
):
    shape = (first_ref.shape[0], BLOCK)
    onehot = lax.broadcasted_iota(jnp.int32, shape, 0) == rows_ref[...]
    table_grad = dot(onehot.astype(F32).astype(BF16), grad_ref[...])
    new_first = BETA_ONE * first_ref[...] + (1.0 - BETA_ONE) * table_grad
    new_second = BETA_TWO * second_ref[...] + (1.0 - BETA_TWO) * table_grad * table_grad
    new_first_ref[...] = new_first
    new_second_ref[...] = new_second
    correct_one = 1.0 - BETA_ONE**ADAM_STEP
    correct_two = 1.0 - BETA_TWO**ADAM_STEP
    direction_ref[...] = new_first / correct_one / (jnp.sqrt(new_second / correct_two) + EPSILON)
    for item in range(CHIPS * CORES):
        for quarter in range(4):
            grad_hidden_ref[item * 16 : item * 16 + 16, quarter * 128 : quarter * 128 + 128] = (
                tower_ref[item, quarter * 16 : quarter * 16 + 16, :].astype(F32)
            )
        grad_embed_ref[item * 32 : item * 32 + 32, :] = tower_ref[item, 64:, :].astype(F32)


def spread(array, copies):
    return jnp.broadcast_to(array[None], (copies, *array.shape))


def swap(array, axes):
    return lax.all_to_all(array, axes, 0, 0, tiled=True)


def main_call(core, states, next_states, rewards, slate_t, chosen, next_slate_t, own, other, w_hidden, w_embed):
    sessions, features = states.shape
    hidden, embed = w_embed.shape
    vmem = pl.BlockSpec(memory_space=pltpu.VMEM)
    return pl.pallas_call(
        main_kernel,
        in_specs=[pl.BlockSpec(memory_space=pltpu.SMEM)] + [vmem] * 10,
        out_specs=[vmem] * 3,
        out_shape=[
            jax.ShapeDtypeStruct((CHIPS, PACK, embed), BF16),
            jax.ShapeDtypeStruct((CHIPS, PACK, embed), BF16),
            jax.ShapeDtypeStruct((1, sessions), F32),
        ],
        scratch_shapes=[
            pltpu.VMEM((hidden, sessions), BF16),
            pltpu.VMEM((embed, sessions), BF16),
            pltpu.VMEM((sessions, embed), BF16),
            pltpu.VMEM((CHIPS * CORES, BLOCK, sessions), F32),
            pltpu.VMEM((CHIPS * CORES * 2, sessions, 128), F32),
            pltpu.VMEM((sessions, 128), jnp.int32),
            pltpu.VMEM((sessions, 128), jnp.int32),
            pltpu.VMEM((sessions, 128), F32),
            pltpu.VMEM((BLOCK, sessions), BF16),
            pltpu.VMEM((features, hidden), F32),
            pltpu.VMEM((hidden, embed), F32),
        ],
        compiler_params=PARAMS,
    )(core, states, next_states, rewards, slate_t, chosen, next_slate_t, own, other, w_hidden, w_embed)


def shards(
    states,
    next_states,
    rewards,
    slate_ids,
    chosen,
    next_slate,
    table,
    first_moment,
    second_moment,
    cand_rows,
    w_hidden,
    w_embed,
):
    embed = table.shape[1]
    sessions = states.shape[0]
    vmem = pl.BlockSpec(memory_space=pltpu.VMEM)
    rows = cand_rows.reshape(1, BLOCK)
    pair = [(0, 1), (1, 0)]

    copies = pl.pallas_call(
        gather_kernel,
        in_specs=[vmem, vmem],
        out_specs=vmem,
        out_shape=jax.ShapeDtypeStruct((CHIPS, BLOCK, embed), BF16),
        compiler_params=PARAMS,
    )(rows, table)
    own = swap(copies, ("x", "l"))
    other = lax.ppermute(own, "c", pair)
    keep, send, delta = main_call(
        lax.axis_index("c").astype(jnp.int32).reshape(1),
        states,
        next_states,
        rewards.reshape(1, sessions),
        slate_ids.T,
        chosen.reshape(1, sessions),
        next_slate.T,
        own,
        other,
        w_hidden,
        w_embed,
    )
    got = lax.ppermute(send, "c", pair)
    part = (keep.astype(F32) + got.astype(F32)).astype(BF16)
    part = jnp.sum(swap(part, ("x", "l")).astype(F32), axis=0)
    part = swap(part.reshape(8, PACK // 8, embed), "z")
    part = jnp.sum(part, axis=0)
    part = jnp.sum(swap(spread(part, 4), "h"), axis=0).astype(BF16)
    whole = swap(spread(part, 8), "z").reshape(PACK, embed)
    tower = swap(spread(whole[BLOCK:], CHIPS * CORES), ITEM)

    moment = jax.ShapeDtypeStruct(first_moment.shape, F32)
    new_first, new_second, direction, grad_hidden, grad_embed = pl.pallas_call(
        adam_kernel,
        in_specs=[vmem] * 5,
        out_specs=[vmem] * 5,
        out_shape=[
            moment,
            moment,
            moment,
            jax.ShapeDtypeStruct(w_hidden.shape, F32),
            jax.ShapeDtypeStruct(w_embed.shape, F32),
        ],
        compiler_params=PARAMS,
    )(rows, whole[:BLOCK], first_moment, second_moment, tower)
    return (new_first, new_second, direction, grad_hidden, grad_embed, delta.reshape(sessions))


def solution(mesh):
    torus = Mesh(mesh.devices.reshape(SIZES), AXES)
    every = P(AXES)
    item = P(ITEM)
    placed = (every,) * 6 + (item,) * 4 + (P(), P())
    return jax.shard_map(
        shards,
        mesh=torus,
        in_specs=placed,
        out_specs=(item, item, item, P(), P(), every),
        check_vma=False,
    )
```

```python
import jax
import jax.numpy as jnp
from jax import lax
from jax.experimental import pallas as pl
from jax.experimental.pallas import tpu as pltpu
from jax.sharding import Mesh
from jax.sharding import PartitionSpec as P

ADAM_STEP = 10
PENALTY = 0.5
DISCOUNT = 0.9
BETA_ONE = 0.9
BETA_TWO = 0.999
EPSILON = 1e-08

AXES = ("h", "z", "x", "l", "c")
SIZES = (4, 8, 4, 2, 2)
ITEM = ("x", "l", "c")
CHIPS = 8
CORES = 2
BLOCK = 256
PACK = 352
DP = 32
PIECE = 12
SLATE = 10
F32 = jnp.float32
BF16 = jnp.bfloat16
NT = (((1,), (1,)), ((), ()))
NN = (((1,), (0,)), ((), ()))
PARAMS = pltpu.CompilerParams(vmem_limit_bytes=48 * 1024 * 1024)


def dot(left, right, dims=NN):
    return lax.dot_general(left, right, dims, preferred_element_type=F32)


def gather_kernel(rows_ref, table_ref, out_ref):
    row = rows_ref[...].astype(F32)
    eye = lax.broadcasted_iota(jnp.int32, (128, 128), 0) == lax.broadcasted_iota(
        jnp.int32, (128, 128), 1
    )
    width = table_ref.shape[0]
    lane = lax.broadcasted_iota(jnp.int32, (128, width), 1).astype(F32)
    onehots = []
    for half in range(BLOCK // 128):
        part = row[:, half * 128 : half * 128 + 128]
        column = jnp.sum(jnp.where(eye, part, 0.0), axis=1, keepdims=True)
        onehots.append((lane == column).astype(F32).astype(BF16))
    table = table_ref[...].astype(BF16)
    for half, onehot in enumerate(onehots):
        slab = dot(onehot, table).astype(BF16)
        for copy in range(out_ref.shape[0]):
            out_ref[copy, half * 128 : half * 128 + 128, :] = slab


def tower_kernel(
    core_ref,
    states_ref,
    next_ref,
    upcoming_ref,
    w_hidden_ref,
    w_embed_ref,
    hidden_t_ref,
    users_t_ref,
    next_users_ref,
    low_ref,
    high_ref,
):
    sessions = states_ref.shape[0]
    w_hidden = w_hidden_ref[...]
    w_embed = w_embed_ref[...]
    hidden_t = jnp.maximum(dot(w_hidden.T, states_ref[...], NT), 0.0).astype(BF16)
    hidden_t_ref[...] = hidden_t
    users_t_ref[...] = dot(w_embed.T, hidden_t).astype(BF16)
    next_hidden = jnp.maximum(dot(next_ref[...], w_hidden), 0.0).astype(BF16)
    next_users_ref[...] = dot(next_hidden, w_embed).astype(BF16)

    upcoming = jnp.bitwise_xor(upcoming_ref[...], core_ref[0] * BLOCK)
    padded = jnp.concatenate(
        [upcoming, jnp.zeros((128 - SLATE, sessions), jnp.int32)], axis=0
    )
    for part in range(sessions // 128):
        rows = slice(part * 128, part * 128 + 128)
        turned = padded[:, rows].astype(F32).T.astype(jnp.int32)
        low_ref[rows, :] = jnp.bitwise_and(turned, 127)
        high_ref[rows, :] = lax.shift_right_logical(turned, 7)


def main_kernel(
    core_ref,
    states_ref,
    hidden_t_ref,
    users_t_ref,
    next_users_ref,
    low_ref,
    high_ref,
    rewards_ref,
    slate_ref,
    chosen_ref,
    own_ref,
    other_ref,
    w_embed_ref,
    keep_ref,
    send_ref,
    delta_ref,
    scores_ref,
    next_scores_ref,
    next_q_ref,
    grad_ref,
    grad_hidden_ref,
    grad_embed_ref,
):
    core = core_ref[0]
    sessions = states_ref.shape[0]
    slabs = (own_ref, other_ref)
    outs = (keep_ref, send_ref)
    w_embed = w_embed_ref[...]

    slate = jnp.bitwise_xor(slate_ref[...], core * BLOCK)
    place = lax.broadcasted_iota(jnp.int32, slate.shape, 0)
    clicked = jnp.sum(jnp.where(place == chosen_ref[...], slate, 0), axis=0, keepdims=True)
    sub = lax.broadcasted_iota(jnp.int32, (8, sessions), 0)
    behind = jnp.broadcast_to(clicked, (8, sessions)) - sub

    def next_forward(chip, _):
        for side in range(CORES):
            block = chip * CORES + side
            next_scores = dot(next_users_ref[...], slabs[side][chip], NT)
            next_scores_ref[block * 2] = next_scores[:, :128]
            next_scores_ref[block * 2 + 1] = next_scores[:, 128:]
        return 0

    lax.fori_loop(0, CHIPS, next_forward, 0, unroll=8)

    groups = sessions // 8 // CHIPS

    def forward(chip, carry):
        highest, picked = carry
        for inner in range(groups):
            rows = pl.ds(pl.multiple_of((chip * groups + inner) * 8, 8), 8)
            low = low_ref[rows, :]
            high = high_ref[rows, :]
            found = jnp.zeros((8, 128), F32)
            for chunk in range(next_scores_ref.shape[0]):
                piece = jnp.take_along_axis(
                    next_scores_ref[chunk, rows, :], low, axis=1, mode="promise_in_bounds"
                )
                found = jnp.where(high == chunk, piece, found)
            next_q_ref[rows, :] = found
        for side in range(CORES):
            block = chip * CORES + side
            scores = dot(slabs[side][chip], users_t_ref[...])
            scores_ref[block] = scores
            first = block * BLOCK
            for step in range(BLOCK // 8):
                piece = scores[step * 8 : step * 8 + 8]
                highest = jnp.maximum(highest, piece)
                picked = picked + jnp.where(behind == first + step * 8, piece, 0.0)
        return highest, picked

    highest, picked = lax.fori_loop(
        0,
        CHIPS,
        forward,
        (jnp.full((8, sessions), -jnp.inf, F32), jnp.zeros((8, sessions), F32)),
        unroll=2,
    )
    highest = jnp.max(highest, axis=0, keepdims=True)
    picked = jnp.sum(picked, axis=0, keepdims=True)

    next_q = jnp.concatenate(
        [next_q_ref[part * 128 : part * 128 + 128, :].T[:16] for part in range(sessions // 128)],
        axis=1,
    )
    shown = lax.broadcasted_iota(jnp.int32, next_q.shape, 0) < SLATE
    top = jnp.max(jnp.where(shown, next_q, -jnp.inf), axis=0, keepdims=True)
    weights = jnp.where(shown, jnp.exp(next_q - top), 0.0)
    mean = jnp.sum(jnp.where(shown, weights * next_q, 0.0), axis=0, keepdims=True) / jnp.sum(
        weights, axis=0, keepdims=True
    )
    delta = picked - (rewards_ref[...] + DISCOUNT * mean)
    delta_ref[...] = delta

    def exponentials(block, total):
        for step in range(BLOCK // 8):
            rows = slice(step * 8, step * 8 + 8)
            piece = jnp.exp(scores_ref[block, rows, :] - highest)
            scores_ref[block, rows, :] = piece
            total = total + piece
        return total

    total = lax.fori_loop(
        0, CHIPS * CORES, exponentials, jnp.zeros((8, sessions), F32), unroll=4
    )
    total = jnp.sum(total, axis=0, keepdims=True)
    scale = 1.0 / sessions
    gain = jnp.broadcast_to((PENALTY * scale) / total, (8, sessions))
    extra = jnp.broadcast_to((delta - PENALTY) * scale, (8, sessions))

    def backward(chip, user_grad_t):
        for side in range(CORES):
            block = chip * CORES + side
            first = block * BLOCK
            for step in range(BLOCK // 16):
                pieces = []
                for inner in range(2):
                    row = step * 16 + inner * 8
                    piece = scores_ref[block, row : row + 8, :] * gain
                    pieces.append(piece + jnp.where(behind == first + row, extra, 0.0))
                grad_ref[step * 16 : step * 16 + 16, :] = jnp.concatenate(pieces, axis=0).astype(
                    BF16
                )
            grad = grad_ref[...]
            slab = slabs[side][chip]
            user_grad_t = user_grad_t + dot(slab.T, grad)
            outs[side][chip, :BLOCK, :] = dot(grad, users_t_ref[...], NT).astype(BF16)
        return user_grad_t

    embed = own_ref.shape[2]
    user_grad_t = lax.fori_loop(
        0, CHIPS, backward, jnp.zeros((embed, sessions), F32), unroll=4
    ).astype(BF16)

    hidden_t = hidden_t_ref[...]
    grad_embed_ref[...] = dot(hidden_t, user_grad_t, NT)
    back = dot(w_embed, user_grad_t)
    pre_grad_t = jnp.where(hidden_t.astype(F32) > 0, back, 0.0).astype(BF16)
    grad_hidden_ref[...] = dot(states_ref[...].T, pre_grad_t, NT)
    for chip in range(CHIPS):
        for side in range(CORES):
            index = chip * CORES + jnp.bitwise_xor(core, side)
            rows = pl.ds(pl.multiple_of(index * 16, 16), 16)
            for quarter in range(4):
                at = BLOCK + quarter * 16
                outs[side][chip, at : at + 16, :] = grad_hidden_ref[
                    rows, quarter * 128 : quarter * 128 + 128
                ].astype(BF16)
            rows = pl.ds(pl.multiple_of(index * 32, 32), 32)
            outs[side][chip, BLOCK + 64 :, :] = grad_embed_ref[rows, :].astype(BF16)


def adam_kernel(
    rows_ref, grad_ref, first_ref, second_ref, new_first_ref, new_second_ref, direction_ref
):
    shape = (first_ref.shape[0], BLOCK)
    onehot = lax.broadcasted_iota(jnp.int32, shape, 0) == rows_ref[...]
    table_grad = dot(onehot.astype(F32).astype(BF16), grad_ref[...])
    new_first = BETA_ONE * first_ref[...] + (1.0 - BETA_ONE) * table_grad
    new_second = BETA_TWO * second_ref[...] + (1.0 - BETA_TWO) * table_grad * table_grad
    new_first_ref[...] = new_first
    new_second_ref[...] = new_second
    correct_one = 1.0 - BETA_ONE**ADAM_STEP
    correct_two = 1.0 - BETA_TWO**ADAM_STEP
    direction_ref[...] = new_first / correct_one / (jnp.sqrt(new_second / correct_two) + EPSILON)


def unpack_kernel(tower_ref, grad_hidden_ref, grad_embed_ref):
    for item in range(CHIPS * CORES):
        for quarter in range(4):
            grad_hidden_ref[item * 16 : item * 16 + 16, quarter * 128 : quarter * 128 + 128] = (
                tower_ref[item, quarter * 16 : quarter * 16 + 16, :].astype(F32)
            )
        grad_embed_ref[item * 32 : item * 32 + 32, :] = tower_ref[item, 64:, :].astype(F32)


def spread(array, copies):
    return jnp.broadcast_to(array[None], (copies, *array.shape))


def swap(array, axes):
    return lax.all_to_all(array, axes, 0, 0, tiled=True)


def tower_call(core, states, next_states, next_slate_t, w_hidden, w_embed):
    sessions = states.shape[0]
    hidden, embed = w_embed.shape
    vmem = pl.BlockSpec(memory_space=pltpu.VMEM)
    places = jax.ShapeDtypeStruct((sessions, 128), jnp.int32)
    return pl.pallas_call(
        tower_kernel,
        in_specs=[pl.BlockSpec(memory_space=pltpu.SMEM)] + [vmem] * 5,
        out_specs=[vmem] * 5,
        out_shape=[
            jax.ShapeDtypeStruct((hidden, sessions), BF16),
            jax.ShapeDtypeStruct((embed, sessions), BF16),
            jax.ShapeDtypeStruct((sessions, embed), BF16),
            places,
            places,
        ],
        compiler_params=PARAMS,
    )(core, states, next_states, next_slate_t, w_hidden, w_embed)


def main_call(core, states, towers, rewards, slate_t, chosen, own, other, w_embed):
    sessions, features = states.shape
    hidden, embed = w_embed.shape
    vmem = pl.BlockSpec(memory_space=pltpu.VMEM)
    return pl.pallas_call(
        main_kernel,
        in_specs=[pl.BlockSpec(memory_space=pltpu.SMEM)] + [vmem] * 12,
        out_specs=[vmem] * 3,
        out_shape=[
            jax.ShapeDtypeStruct((CHIPS, PACK, embed), BF16),
            jax.ShapeDtypeStruct((CHIPS, PACK, embed), BF16),
            jax.ShapeDtypeStruct((1, sessions), F32),
        ],
        scratch_shapes=[
            pltpu.VMEM((CHIPS * CORES, BLOCK, sessions), F32),
            pltpu.VMEM((CHIPS * CORES * 2, sessions, 128), F32),
            pltpu.VMEM((sessions, 128), F32),
            pltpu.VMEM((BLOCK, sessions), BF16),
            pltpu.VMEM((features, hidden), F32),
            pltpu.VMEM((hidden, embed), F32),
        ],
        compiler_params=PARAMS,
    )(core, states, *towers, rewards, slate_t, chosen, own, other, w_embed)


def shards(
    states,
    next_states,
    rewards,
    slate_ids,
    chosen,
    next_slate,
    table,
    first_moment,
    second_moment,
    cand_rows,
    w_hidden,
    w_embed,
):
    embed = table.shape[1]
    sessions = states.shape[0]
    vmem = pl.BlockSpec(memory_space=pltpu.VMEM)
    rows = cand_rows.reshape(1, BLOCK)
    pair = [(0, 1), (1, 0)]

    copies = pl.pallas_call(
        gather_kernel,
        in_specs=[vmem] * 2,
        out_specs=vmem,
        out_shape=jax.ShapeDtypeStruct((CHIPS, BLOCK, embed), BF16),
        compiler_params=PARAMS,
    )(rows, table)
    core = lax.axis_index("c").astype(jnp.int32).reshape(1)
    towers = tower_call(core, states, next_states, next_slate.T, w_hidden, w_embed)
    own = swap(copies, ("x", "l"))
    other = lax.ppermute(own, "c", pair)
    keep, send, delta = main_call(
        core,
        states,
        towers,
        rewards.reshape(1, sessions),
        slate_ids.T,
        chosen.reshape(1, sessions),
        own,
        other,
        w_embed,
    )

    got = lax.ppermute(send, "c", pair)
    part = (keep.astype(F32) + got.astype(F32)).astype(BF16)
    part = jnp.sum(swap(part, ("x", "l")).astype(F32), axis=0)
    part = jnp.pad(part, ((0, PIECE * DP - PACK), (0, 0))).reshape(DP, PIECE, embed)
    part = jnp.sum(swap(part, ("h", "z")), axis=0).astype(BF16)
    whole = swap(spread(part, DP), ("h", "z")).reshape(DP * PIECE, embed)
    tower = swap(spread(whole[BLOCK:PACK], CHIPS * CORES), ITEM)

    moment = jax.ShapeDtypeStruct(first_moment.shape, F32)
    new_first, new_second, direction = pl.pallas_call(
        adam_kernel,
        in_specs=[vmem] * 4,
        out_specs=[vmem] * 3,
        out_shape=[moment, moment, moment],
        compiler_params=PARAMS,
    )(rows, whole[:BLOCK], first_moment, second_moment)
    grad_hidden, grad_embed = pl.pallas_call(
        unpack_kernel,
        in_specs=[vmem],
        out_specs=[vmem] * 2,
        out_shape=[
            jax.ShapeDtypeStruct(w_hidden.shape, F32),
            jax.ShapeDtypeStruct(w_embed.shape, F32),
        ],
        compiler_params=PARAMS,
    )(tower)
    return (new_first, new_second, direction, grad_hidden, grad_embed, delta.reshape(sessions))


def solution(mesh):
    torus = Mesh(mesh.devices.reshape(SIZES), AXES)
    every = P(AXES)
    item = P(ITEM)
    placed = (every,) * 6 + (item,) * 4 + (P(), P())
    return jax.shard_map(
        shards,
        mesh=torus,
        in_specs=placed,
        out_specs=(item, item, item, P(), P(), every),
        check_vma=False,
    )
```

```python
import jax
import jax.numpy as jnp
from jax import lax
from jax.experimental import pallas as pl
from jax.experimental.pallas import tpu as pltpu
from jax.sharding import Mesh
from jax.sharding import PartitionSpec as P

ADAM_STEP = 10
PENALTY = 0.5
DISCOUNT = 0.9
BETA_ONE = 0.9
BETA_TWO = 0.999
EPSILON = 1e-08

AXES = ("h", "z", "x", "l", "c")
SIZES = (4, 8, 4, 2, 2)
ITEM = ("x", "l", "c")
CHIPS = 8
CORES = 2
BLOCK = 256
PACK = 352
DP = 32
PIECE = 16
TOWER_PIECES = (PACK - BLOCK) // 8
SLATE = 10
F32 = jnp.float32
BF16 = jnp.bfloat16
NT = (((1,), (1,)), ((), ()))
NN = (((1,), (0,)), ((), ()))
PARAMS = pltpu.CompilerParams(vmem_limit_bytes=48 * 1024 * 1024)


def dot(left, right, dims=NN):
    return lax.dot_general(left, right, dims, preferred_element_type=F32)


def gather_kernel(rows_ref, table_ref, out_ref):
    row = rows_ref[...].astype(F32)
    eye = lax.broadcasted_iota(jnp.int32, (128, 128), 0) == lax.broadcasted_iota(
        jnp.int32, (128, 128), 1
    )
    width = table_ref.shape[0]
    lane = lax.broadcasted_iota(jnp.int32, (128, width), 1).astype(F32)
    onehots = []
    for half in range(BLOCK // 128):
        part = row[:, half * 128 : half * 128 + 128]
        column = jnp.sum(jnp.where(eye, part, 0.0), axis=1, keepdims=True)
        onehots.append((lane == column).astype(F32).astype(BF16))
    table = table_ref[...].astype(BF16)
    for half, onehot in enumerate(onehots):
        slab = dot(onehot, table).astype(BF16)
        for copy in range(out_ref.shape[0]):
            out_ref[copy, half * 128 : half * 128 + 128, :] = slab


def tower_kernel(
    core_ref,
    states_ref,
    next_ref,
    upcoming_ref,
    w_hidden_ref,
    w_embed_ref,
    hidden_t_ref,
    users_t_ref,
    next_users_ref,
    low_ref,
    high_ref,
):
    sessions = states_ref.shape[0]
    w_hidden = w_hidden_ref[...]
    w_embed = w_embed_ref[...]
    hidden_t = jnp.maximum(dot(w_hidden.T, states_ref[...], NT), 0.0).astype(BF16)
    hidden_t_ref[...] = hidden_t
    users_t_ref[...] = dot(w_embed.T, hidden_t).astype(BF16)
    next_hidden = jnp.maximum(dot(next_ref[...], w_hidden), 0.0).astype(BF16)
    next_users_ref[...] = dot(next_hidden, w_embed).astype(BF16)

    upcoming = jnp.bitwise_xor(upcoming_ref[...], core_ref[0] * BLOCK)
    padded = jnp.concatenate(
        [upcoming, jnp.zeros((128 - SLATE, sessions), jnp.int32)], axis=0
    )
    for part in range(sessions // 128):
        rows = slice(part * 128, part * 128 + 128)
        turned = padded[:, rows].astype(F32).T.astype(jnp.int32)
        low_ref[rows, :] = jnp.bitwise_and(turned, 127)
        high_ref[rows, :] = lax.shift_right_logical(turned, 7)


def main_kernel(
    core_ref,
    states_ref,
    hidden_t_ref,
    users_t_ref,
    next_users_ref,
    low_ref,
    high_ref,
    rewards_ref,
    slate_ref,
    chosen_ref,
    own_ref,
    other_ref,
    w_embed_ref,
    keep_ref,
    send_ref,
    delta_ref,
    scores_ref,
    next_scores_ref,
    next_q_ref,
    grad_ref,
    grad_hidden_ref,
    grad_embed_ref,
):
    core = core_ref[0]
    sessions = states_ref.shape[0]
    slabs = (own_ref, other_ref)
    outs = (keep_ref, send_ref)
    w_embed = w_embed_ref[...]

    slate = jnp.bitwise_xor(slate_ref[...], core * BLOCK)
    place = lax.broadcasted_iota(jnp.int32, slate.shape, 0)
    clicked = jnp.sum(jnp.where(place == chosen_ref[...], slate, 0), axis=0, keepdims=True)
    sub = lax.broadcasted_iota(jnp.int32, (8, sessions), 0)
    behind = jnp.broadcast_to(clicked, (8, sessions)) - sub

    blocks = [(chip, side) for chip in range(CHIPS) for side in range(CORES)]
    next_users = next_users_ref[...]
    for block, (chip, side) in enumerate(blocks):
        next_scores = dot(next_users, slabs[side][chip], NT)
        next_scores_ref[block * 2] = next_scores[:, :128]
        next_scores_ref[block * 2 + 1] = next_scores[:, 128:]

    highest = jnp.full((8, sessions), -jnp.inf, F32)
    picked = jnp.zeros((8, sessions), F32)
    groups = sessions // 8 // len(blocks)
    for block, (chip, side) in enumerate(blocks):
        for group in range(block * groups, (block + 1) * groups):
            rows = slice(group * 8, group * 8 + 8)
            low = low_ref[rows, :]
            high = high_ref[rows, :]
            found = jnp.zeros((8, 128), F32)
            for chunk in range(next_scores_ref.shape[0]):
                piece = jnp.take_along_axis(
                    next_scores_ref[chunk, rows, :], low, axis=1, mode="promise_in_bounds"
                )
                found = jnp.where(high == chunk, piece, found)
            next_q_ref[rows, :] = found
        scores = dot(slabs[side][chip], users_t_ref[...])
        scores_ref[block] = scores
        for step in range(BLOCK // 8):
            piece = scores[step * 8 : step * 8 + 8]
            highest = jnp.maximum(highest, piece)
            picked = jnp.where(behind == block * BLOCK + step * 8, piece, picked)
    highest = jnp.max(highest, axis=0, keepdims=True)
    picked = jnp.sum(picked, axis=0, keepdims=True)

    next_q = jnp.concatenate(
        [next_q_ref[part * 128 : part * 128 + 128, :].T[:16] for part in range(sessions // 128)],
        axis=1,
    )
    shown = lax.broadcasted_iota(jnp.int32, next_q.shape, 0) < SLATE
    top = jnp.max(jnp.where(shown, next_q, -jnp.inf), axis=0, keepdims=True)
    weights = jnp.where(shown, jnp.exp(next_q - top), 0.0)
    mean = jnp.sum(jnp.where(shown, weights * next_q, 0.0), axis=0, keepdims=True) / jnp.sum(
        weights, axis=0, keepdims=True
    )
    delta = picked - (rewards_ref[...] + DISCOUNT * mean)
    delta_ref[...] = delta

    def exponentials(block, total):
        for step in range(BLOCK // 8):
            rows = slice(step * 8, step * 8 + 8)
            piece = jnp.exp(scores_ref[block, rows, :] - highest)
            scores_ref[block, rows, :] = piece
            total = total + piece
        return total

    total = lax.fori_loop(
        0, CHIPS * CORES, exponentials, jnp.zeros((8, sessions), F32), unroll=8
    )
    total = jnp.sum(total, axis=0, keepdims=True)
    scale = 1.0 / sessions
    gain = jnp.broadcast_to((PENALTY * scale) / total, (8, sessions))
    extra = jnp.broadcast_to((delta - PENALTY) * scale, (8, sessions))

    user_grad_t = jnp.zeros((own_ref.shape[2], sessions), F32)
    for block, (chip, side) in enumerate(blocks):
        for step in range(BLOCK // 16):
            pieces = []
            for inner in range(2):
                row = step * 16 + inner * 8
                piece = scores_ref[block, row : row + 8, :] * gain
                pieces.append(
                    piece + jnp.where(behind == block * BLOCK + row, extra, 0.0)
                )
            grad_ref[block, step * 16 : step * 16 + 16, :] = jnp.concatenate(
                pieces, axis=0
            ).astype(BF16)
        grad = grad_ref[block]
        slab = slabs[side][chip]
        user_grad_t = user_grad_t + dot(slab.T, grad)
        outs[side][chip, :BLOCK, :] = dot(grad, users_t_ref[...], NT).astype(outs[side].dtype)
    user_grad_t = user_grad_t.astype(BF16)

    hidden_t = hidden_t_ref[...]
    grad_embed_ref[...] = dot(hidden_t, user_grad_t, NT)
    back = dot(w_embed, user_grad_t)
    pre_grad_t = jnp.where(hidden_t.astype(F32) > 0, back, 0.0).astype(BF16)
    grad_hidden_ref[...] = dot(states_ref[...].T, pre_grad_t, NT)
    for chip in range(CHIPS):
        for side in range(CORES):
            index = chip * CORES + jnp.bitwise_xor(core, side)
            rows = pl.ds(pl.multiple_of(index * 16, 16), 16)
            for quarter in range(4):
                at = BLOCK + quarter * 16
                outs[side][chip, at : at + 16, :] = grad_hidden_ref[
                    rows, quarter * 128 : quarter * 128 + 128
                ].astype(outs[side].dtype)
            rows = pl.ds(pl.multiple_of(index * 32, 32), 32)
            outs[side][chip, BLOCK + 64 :, :] = grad_embed_ref[rows, :].astype(outs[side].dtype)


def cut_kernel(parts_ref, out_ref):
    def total(first):
        rows = slice(first, first + 16)
        return sum(parts_ref[chip, rows, :].astype(F32) for chip in range(parts_ref.shape[0]))

    towers = []
    for first in range(BLOCK, PACK, 16):
        both = total(first)
        towers += [both[:8], both[8:]]
    for first in range(0, BLOCK, 16):
        both = total(first)
        for inner in range(2):
            piece = first // 8 + inner
            tower = towers[piece] if piece < TOWER_PIECES else jnp.zeros_like(both[:8])
            out_ref[piece] = jnp.concatenate(
                [both[inner * 8 : inner * 8 + 8], tower], axis=0
            ).astype(BF16)


def piece_kernel(parts_ref, out_ref):
    total = sum(parts_ref[part].astype(F32) for part in range(parts_ref.shape[0])).astype(BF16)
    for copy in range(out_ref.shape[0]):
        out_ref[copy] = total


def tower_copies_kernel(pieces_ref, out_ref):
    rows = jnp.concatenate(
        [pieces_ref[piece].astype(F32)[8:] for piece in range(TOWER_PIECES)], axis=0
    ).astype(BF16)
    for copy in range(out_ref.shape[0]):
        out_ref[copy] = rows


def adam_kernel(
    rows_ref, pieces_ref, first_ref, second_ref, new_first_ref, new_second_ref, direction_ref
):
    shape = (first_ref.shape[0], BLOCK)
    onehot = lax.broadcasted_iota(jnp.int32, shape, 0) == rows_ref[...]
    grad = jnp.concatenate([pieces_ref[piece].astype(F32)[:8] for piece in range(DP)], axis=0)
    table_grad = dot(onehot.astype(F32).astype(BF16), grad.astype(BF16))
    new_first = BETA_ONE * first_ref[...] + (1.0 - BETA_ONE) * table_grad
    new_second = BETA_TWO * second_ref[...] + (1.0 - BETA_TWO) * table_grad * table_grad
    new_first_ref[...] = new_first
    new_second_ref[...] = new_second
    correct_one = 1.0 - BETA_ONE**ADAM_STEP
    correct_two = 1.0 - BETA_TWO**ADAM_STEP
    direction_ref[...] = new_first / correct_one / (jnp.sqrt(new_second / correct_two) + EPSILON)


def unpack_kernel(tower_ref, grad_hidden_ref, grad_embed_ref):
    for item in range(CHIPS * CORES):
        for quarter in range(4):
            grad_hidden_ref[item * 16 : item * 16 + 16, quarter * 128 : quarter * 128 + 128] = (
                tower_ref[item, quarter * 16 : quarter * 16 + 16, :].astype(F32)
            )
        grad_embed_ref[item * 32 : item * 32 + 32, :] = tower_ref[item, 64:, :].astype(F32)


def in_vmem(kernel, array, shape):
    vmem = pl.BlockSpec(memory_space=pltpu.VMEM)
    return pl.pallas_call(
        kernel,
        in_specs=[vmem],
        out_specs=vmem,
        out_shape=jax.ShapeDtypeStruct(shape, BF16),
        compiler_params=PARAMS,
    )(array)


def swap(array, axes):
    return lax.all_to_all(array, axes, 0, 0, tiled=True)


def tower_call(core, states, next_states, next_slate_t, w_hidden, w_embed):
    sessions = states.shape[0]
    hidden, embed = w_embed.shape
    vmem = pl.BlockSpec(memory_space=pltpu.VMEM)
    places = jax.ShapeDtypeStruct((sessions, 128), jnp.int32)
    return pl.pallas_call(
        tower_kernel,
        in_specs=[pl.BlockSpec(memory_space=pltpu.SMEM)] + [vmem] * 5,
        out_specs=[vmem] * 5,
        out_shape=[
            jax.ShapeDtypeStruct((hidden, sessions), BF16),
            jax.ShapeDtypeStruct((embed, sessions), BF16),
            jax.ShapeDtypeStruct((sessions, embed), BF16),
            places,
            places,
        ],
        compiler_params=PARAMS,
    )(core, states, next_states, next_slate_t, w_hidden, w_embed)


def main_call(core, states, towers, rewards, slate_t, chosen, own, other, w_embed):
    sessions, features = states.shape
    hidden, embed = w_embed.shape
    vmem = pl.BlockSpec(memory_space=pltpu.VMEM)
    return pl.pallas_call(
        main_kernel,
        in_specs=[pl.BlockSpec(memory_space=pltpu.SMEM)] + [vmem] * 12,
        out_specs=[vmem] * 3,
        out_shape=[
            jax.ShapeDtypeStruct((CHIPS, PACK, embed), F32),
            jax.ShapeDtypeStruct((CHIPS, PACK, embed), BF16),
            jax.ShapeDtypeStruct((1, sessions), F32),
        ],
        scratch_shapes=[
            pltpu.VMEM((CHIPS * CORES, BLOCK, sessions), F32),
            pltpu.VMEM((CHIPS * CORES * 2, sessions, 128), F32),
            pltpu.VMEM((sessions, 128), F32),
            pltpu.VMEM((CHIPS * CORES, BLOCK, sessions), BF16),
            pltpu.VMEM((features, hidden), F32),
            pltpu.VMEM((hidden, embed), F32),
        ],
        compiler_params=PARAMS,
    )(core, states, *towers, rewards, slate_t, chosen, own, other, w_embed)


def shards(
    states,
    next_states,
    rewards,
    slate_ids,
    chosen,
    next_slate,
    table,
    first_moment,
    second_moment,
    cand_rows,
    w_hidden,
    w_embed,
):
    embed = table.shape[1]
    sessions = states.shape[0]
    vmem = pl.BlockSpec(memory_space=pltpu.VMEM)
    rows = cand_rows.reshape(1, BLOCK)
    pair = [(0, 1), (1, 0)]

    copies = pl.pallas_call(
        gather_kernel,
        in_specs=[vmem] * 2,
        out_specs=vmem,
        out_shape=jax.ShapeDtypeStruct((CHIPS, BLOCK, embed), BF16),
        compiler_params=PARAMS,
    )(rows, table)
    core = lax.axis_index("c").astype(jnp.int32).reshape(1)
    towers = tower_call(core, states, next_states, next_slate.T, w_hidden, w_embed)
    own = swap(copies, ("x", "l"))
    other = lax.ppermute(own, "c", pair)
    keep, send, delta = main_call(
        core,
        states,
        towers,
        rewards.reshape(1, sessions),
        slate_ids.T,
        chosen.reshape(1, sessions),
        own,
        other,
        w_embed,
    )

    got = lax.ppermute(send, "c", pair)
    part = (keep + got.astype(F32)).astype(BF16)
    pieces = in_vmem(cut_kernel, swap(part, ("x", "l")), (DP, PIECE, embed))
    pieces = in_vmem(piece_kernel, swap(pieces, ("h", "z")), (DP, PIECE, embed))
    pieces = swap(pieces, ("h", "z"))
    tower = in_vmem(tower_copies_kernel, pieces, (CHIPS * CORES, PACK - BLOCK, embed))
    tower = swap(tower, ITEM)

    moment = jax.ShapeDtypeStruct(first_moment.shape, F32)
    new_first, new_second, direction = pl.pallas_call(
        adam_kernel,
        in_specs=[vmem] * 4,
        out_specs=[vmem] * 3,
        out_shape=[moment, moment, moment],
        compiler_params=PARAMS,
    )(rows, pieces, first_moment, second_moment)
    grad_hidden, grad_embed = pl.pallas_call(
        unpack_kernel,
        in_specs=[vmem],
        out_specs=[vmem] * 2,
        out_shape=[
            jax.ShapeDtypeStruct(w_hidden.shape, F32),
            jax.ShapeDtypeStruct(w_embed.shape, F32),
        ],
        compiler_params=PARAMS,
    )(tower)
    return (new_first, new_second, direction, grad_hidden, grad_embed, delta.reshape(sessions))


def solution(mesh):
    torus = Mesh(mesh.devices.reshape(SIZES), AXES)
    every = P(AXES)
    item = P(ITEM)
    placed = (every,) * 6 + (item,) * 4 + (P(), P())
    return jax.shard_map(
        shards,
        mesh=torus,
        in_specs=placed,
        out_specs=(item, item, item, P(), P(), every),
        check_vma=False,
    )
```

```python
import jax
import jax.numpy as jnp
from jax import lax
from jax.experimental import pallas as pl
from jax.experimental.pallas import tpu as pltpu
from jax.sharding import Mesh
from jax.sharding import PartitionSpec as P

ADAM_STEP = 10
PENALTY = 0.5
DISCOUNT = 0.9
BETA_ONE = 0.9
BETA_TWO = 0.999
EPSILON = 1e-08

AXES = ("h", "z", "x", "l", "c")
SIZES = (4, 8, 4, 2, 2)
ITEM = ("x", "l", "c")
Y = ("h", "l")
XZ = ("z", "x")
CHIPS = 8
CORES = 2
BLOCK = 256
PLANE = 32
EIGHTH = BLOCK // 8
TOWER = 32
SLATE = 10
F32 = jnp.float32
BF16 = jnp.bfloat16
NT = (((1,), (1,)), ((), ()))
NN = (((1,), (0,)), ((), ()))
PARAMS = pltpu.CompilerParams(vmem_limit_bytes=48 * 1024 * 1024)


def dot(left, right, dims=NN):
    return lax.dot_general(left, right, dims, preferred_element_type=F32)


def gather_kernel(rows_ref, table_ref, out_ref):
    row = rows_ref[...].astype(F32)
    eye = lax.broadcasted_iota(jnp.int32, (128, 128), 0) == lax.broadcasted_iota(
        jnp.int32, (128, 128), 1
    )
    width = table_ref.shape[0]
    lane = lax.broadcasted_iota(jnp.int32, (128, width), 1).astype(F32)
    onehots = []
    for half in range(BLOCK // 128):
        part = row[:, half * 128 : half * 128 + 128]
        column = jnp.sum(jnp.where(eye, part, 0.0), axis=1, keepdims=True)
        onehots.append((lane == column).astype(F32).astype(BF16))
    table = table_ref[...].astype(BF16)
    for half, onehot in enumerate(onehots):
        slab = dot(onehot, table).astype(BF16)
        for copy in range(out_ref.shape[0]):
            out_ref[copy, half * 128 : half * 128 + 128, :] = slab


def tower_kernel(
    core_ref,
    states_ref,
    next_ref,
    upcoming_ref,
    w_hidden_ref,
    w_embed_ref,
    hidden_t_ref,
    users_t_ref,
    next_users_ref,
    low_ref,
    high_ref,
):
    sessions = states_ref.shape[0]
    w_hidden = w_hidden_ref[...]
    w_embed = w_embed_ref[...]
    hidden_t = jnp.maximum(dot(w_hidden.T, states_ref[...], NT), 0.0).astype(BF16)
    hidden_t_ref[...] = hidden_t
    users_t_ref[...] = dot(w_embed.T, hidden_t).astype(BF16)
    next_hidden = jnp.maximum(dot(next_ref[...], w_hidden), 0.0).astype(BF16)
    next_users_ref[...] = dot(next_hidden, w_embed).astype(BF16)

    upcoming = jnp.bitwise_xor(upcoming_ref[...], core_ref[0] * BLOCK)
    padded = jnp.concatenate(
        [upcoming, jnp.zeros((128 - SLATE, sessions), jnp.int32)], axis=0
    )
    for part in range(sessions // 128):
        rows = slice(part * 128, part * 128 + 128)
        turned = padded[:, rows].astype(F32).T.astype(jnp.int32)
        low_ref[rows, :] = jnp.bitwise_and(turned, 127)
        high_ref[rows, :] = lax.shift_right_logical(turned, 7)


def main_kernel(
    core_ref,
    states_ref,
    hidden_t_ref,
    users_t_ref,
    next_users_ref,
    low_ref,
    high_ref,
    rewards_ref,
    slate_ref,
    chosen_ref,
    own_ref,
    other_ref,
    w_embed_ref,
    keep_ref,
    send_ref,
    delta_ref,
    scores_ref,
    next_scores_ref,
    next_q_ref,
    grad_ref,
    grad_hidden_ref,
    grad_embed_ref,
):
    core = core_ref[0]
    sessions = states_ref.shape[0]
    slabs = (own_ref, other_ref)
    outs = (keep_ref, send_ref)
    w_embed = w_embed_ref[...]

    slate = jnp.bitwise_xor(slate_ref[...], core * BLOCK)
    place = lax.broadcasted_iota(jnp.int32, slate.shape, 0)
    clicked = jnp.sum(jnp.where(place == chosen_ref[...], slate, 0), axis=0, keepdims=True)
    sub = lax.broadcasted_iota(jnp.int32, (8, sessions), 0)
    behind = jnp.broadcast_to(clicked, (8, sessions)) - sub

    blocks = [(chip, side) for chip in range(CHIPS) for side in range(CORES)]
    next_users = next_users_ref[...]
    for block, (chip, side) in enumerate(blocks):
        next_scores = dot(next_users, slabs[side][chip], NT)
        next_scores_ref[block * 2] = next_scores[:, :128]
        next_scores_ref[block * 2 + 1] = next_scores[:, 128:]

    highest = jnp.full((8, sessions), -jnp.inf, F32)
    picked = jnp.zeros((8, sessions), F32)
    groups = sessions // 8 // len(blocks)
    for block, (chip, side) in enumerate(blocks):
        for group in range(block * groups, (block + 1) * groups):
            rows = slice(group * 8, group * 8 + 8)
            low = low_ref[rows, :]
            high = high_ref[rows, :]
            found = jnp.zeros((8, 128), F32)
            for chunk in range(next_scores_ref.shape[0]):
                piece = jnp.take_along_axis(
                    next_scores_ref[chunk, rows, :], low, axis=1, mode="promise_in_bounds"
                )
                found = jnp.where(high == chunk, piece, found)
            next_q_ref[rows, :] = found
        scores = dot(slabs[side][chip], users_t_ref[...])
        scores_ref[block] = scores
        for step in range(BLOCK // 8):
            piece = scores[step * 8 : step * 8 + 8]
            highest = jnp.maximum(highest, piece)
            picked = jnp.where(behind == block * BLOCK + step * 8, piece, picked)
    highest = jnp.max(highest, axis=0, keepdims=True)
    picked = jnp.sum(picked, axis=0, keepdims=True)

    next_q = jnp.concatenate(
        [next_q_ref[part * 128 : part * 128 + 128, :].T[:16] for part in range(sessions // 128)],
        axis=1,
    )
    shown = lax.broadcasted_iota(jnp.int32, next_q.shape, 0) < SLATE
    top = jnp.max(jnp.where(shown, next_q, -jnp.inf), axis=0, keepdims=True)
    weights = jnp.where(shown, jnp.exp(next_q - top), 0.0)
    mean = jnp.sum(jnp.where(shown, weights * next_q, 0.0), axis=0, keepdims=True) / jnp.sum(
        weights, axis=0, keepdims=True
    )
    delta = picked - (rewards_ref[...] + DISCOUNT * mean)
    delta_ref[...] = delta

    def exponentials(block, total):
        for step in range(BLOCK // 8):
            rows = slice(step * 8, step * 8 + 8)
            piece = jnp.exp(scores_ref[block, rows, :] - highest)
            scores_ref[block, rows, :] = piece
            total = total + piece
        return total

    total = lax.fori_loop(
        0, CHIPS * CORES, exponentials, jnp.zeros((8, sessions), F32), unroll=8
    )
    total = jnp.sum(total, axis=0, keepdims=True)
    scale = 1.0 / sessions
    gain = jnp.broadcast_to((PENALTY * scale) / total, (8, sessions))
    extra = jnp.broadcast_to((delta - PENALTY) * scale, (8, sessions))

    user_grad_t = jnp.zeros((own_ref.shape[2], sessions), F32)
    for block, (chip, side) in enumerate(blocks):
        for step in range(BLOCK // 16):
            pieces = []
            for inner in range(2):
                row = step * 16 + inner * 8
                piece = scores_ref[block, row : row + 8, :] * gain
                pieces.append(
                    piece + jnp.where(behind == block * BLOCK + row, extra, 0.0)
                )
            grad_ref[block, step * 16 : step * 16 + 16, :] = jnp.concatenate(
                pieces, axis=0
            ).astype(BF16)
        grad = grad_ref[block]
        slab = slabs[side][chip]
        user_grad_t = user_grad_t + dot(slab.T, grad)
        slab_grad = dot(grad, users_t_ref[...], NT).astype(outs[side].dtype)
        at = chip % 2 * EIGHTH
        for z in range(8):
            outs[side][z * 4 + chip // 2, at : at + EIGHTH, :] = slab_grad[
                z * EIGHTH : z * EIGHTH + EIGHTH
            ]
    user_grad_t = user_grad_t.astype(BF16)

    hidden_t = hidden_t_ref[...]
    grad_embed_ref[...] = dot(hidden_t, user_grad_t, NT)
    back = dot(w_embed, user_grad_t)
    pre_grad_t = jnp.where(hidden_t.astype(F32) > 0, back, 0.0).astype(BF16)
    grad_hidden_ref[...] = dot(states_ref[...].T, pre_grad_t, NT)
    for side in range(CORES):
        half = jnp.bitwise_xor(core, side)
        for piece in range(PLANE):
            quarter, part = piece // 8, piece % 8
            rows = pl.ds(pl.multiple_of(half * 128 + part * 16, 16), 16)
            outs[side][piece, 2 * EIGHTH : 2 * EIGHTH + 16, :] = grad_hidden_ref[
                rows, quarter * 128 : quarter * 128 + 128
            ].astype(outs[side].dtype)
            rows = pl.ds(pl.multiple_of(half * 256 + piece * 8, 8), 8)
            outs[side][piece, 2 * EIGHTH + 16 :, :] = jnp.concatenate(
                [grad_embed_ref[rows, :], jnp.zeros((8, 128), F32)], axis=0
            ).astype(outs[side].dtype)


def plane_kernel(parts_ref, out_ref):
    total = sum(parts_ref[part].astype(F32) for part in range(parts_ref.shape[0])).astype(BF16)
    for to in range(out_ref.shape[0]):
        at = to % 2 * EIGHTH
        out_ref[to, :EIGHTH, :] = total[at : at + EIGHTH]
        out_ref[to, EIGHTH:, :] = total[2 * EIGHTH :]


def line_kernel(parts_ref, out_ref):
    total = sum(parts_ref[part].astype(F32) for part in range(parts_ref.shape[0])).astype(BF16)
    for copy in range(out_ref.shape[0]):
        out_ref[copy] = total


def adam_kernel(
    x_ref, rows_ref, pieces_ref, first_ref, second_ref, new_first_ref, new_second_ref, direction_ref
):
    shape = (first_ref.shape[0], BLOCK)
    onehot = lax.broadcasted_iota(jnp.int32, shape, 0) == rows_ref[...]
    grad = jnp.concatenate([pieces_ref[z * 4 + x_ref[0], :EIGHTH, :] for z in range(8)], axis=0)
    table_grad = dot(onehot.astype(F32).astype(BF16), grad)
    new_first = BETA_ONE * first_ref[...] + (1.0 - BETA_ONE) * table_grad
    new_second = BETA_TWO * second_ref[...] + (1.0 - BETA_TWO) * table_grad * table_grad
    new_first_ref[...] = new_first
    new_second_ref[...] = new_second
    correct_one = 1.0 - BETA_ONE**ADAM_STEP
    correct_two = 1.0 - BETA_TWO**ADAM_STEP
    direction_ref[...] = new_first / correct_one / (jnp.sqrt(new_second / correct_two) + EPSILON)


def unpack_kernel(core_ref, own_ref, other_ref, grad_hidden_ref, grad_embed_ref):
    for side, pieces_ref in enumerate((own_ref, other_ref)):
        half = jnp.bitwise_xor(core_ref[0], side)
        for piece in range(PLANE):
            quarter, part = piece // 8, piece % 8
            rows = pl.ds(pl.multiple_of(half * 128 + part * 16, 16), 16)
            grad_hidden_ref[rows, quarter * 128 : quarter * 128 + 128] = pieces_ref[
                piece, EIGHTH : EIGHTH + 16, :
            ].astype(F32)
            rows = pl.ds(pl.multiple_of(half * 256 + piece * 8, 8), 8)
            grad_embed_ref[rows, :] = pieces_ref[piece, EIGHTH + 16 :, :].astype(F32)[:8]


def in_vmem(kernel, array, shape):
    vmem = pl.BlockSpec(memory_space=pltpu.VMEM)
    return pl.pallas_call(
        kernel,
        in_specs=[vmem],
        out_specs=vmem,
        out_shape=jax.ShapeDtypeStruct(shape, BF16),
        compiler_params=PARAMS,
    )(array)


def swap(array, axes):
    return lax.all_to_all(array, axes, 0, 0, tiled=True)


def tower_call(core, states, next_states, next_slate_t, w_hidden, w_embed):
    sessions = states.shape[0]
    hidden, embed = w_embed.shape
    vmem = pl.BlockSpec(memory_space=pltpu.VMEM)
    places = jax.ShapeDtypeStruct((sessions, 128), jnp.int32)
    return pl.pallas_call(
        tower_kernel,
        in_specs=[pl.BlockSpec(memory_space=pltpu.SMEM)] + [vmem] * 5,
        out_specs=[vmem] * 5,
        out_shape=[
            jax.ShapeDtypeStruct((hidden, sessions), BF16),
            jax.ShapeDtypeStruct((embed, sessions), BF16),
            jax.ShapeDtypeStruct((sessions, embed), BF16),
            places,
            places,
        ],
        compiler_params=PARAMS,
    )(core, states, next_states, next_slate_t, w_hidden, w_embed)


def main_call(core, states, towers, rewards, slate_t, chosen, own, other, w_embed):
    sessions, features = states.shape
    hidden, embed = w_embed.shape
    vmem = pl.BlockSpec(memory_space=pltpu.VMEM)
    return pl.pallas_call(
        main_kernel,
        in_specs=[pl.BlockSpec(memory_space=pltpu.SMEM)] + [vmem] * 12,
        out_specs=[vmem] * 3,
        out_shape=[
            jax.ShapeDtypeStruct((PLANE, 2 * EIGHTH + TOWER, embed), F32),
            jax.ShapeDtypeStruct((PLANE, 2 * EIGHTH + TOWER, embed), BF16),
            jax.ShapeDtypeStruct((1, sessions), F32),
        ],
        scratch_shapes=[
            pltpu.VMEM((CHIPS * CORES, BLOCK, sessions), F32),
            pltpu.VMEM((CHIPS * CORES * 2, sessions, 128), F32),
            pltpu.VMEM((sessions, 128), F32),
            pltpu.VMEM((CHIPS * CORES, BLOCK, sessions), BF16),
            pltpu.VMEM((features, hidden), F32),
            pltpu.VMEM((hidden, embed), F32),
        ],
        compiler_params=PARAMS,
    )(core, states, *towers, rewards, slate_t, chosen, own, other, w_embed)


def shards(
    states,
    next_states,
    rewards,
    slate_ids,
    chosen,
    next_slate,
    table,
    first_moment,
    second_moment,
    cand_rows,
    w_hidden,
    w_embed,
):
    embed = table.shape[1]
    sessions = states.shape[0]
    vmem = pl.BlockSpec(memory_space=pltpu.VMEM)
    rows = cand_rows.reshape(1, BLOCK)
    pair = [(0, 1), (1, 0)]

    copies = pl.pallas_call(
        gather_kernel,
        in_specs=[vmem] * 2,
        out_specs=vmem,
        out_shape=jax.ShapeDtypeStruct((CHIPS, BLOCK, embed), BF16),
        compiler_params=PARAMS,
    )(rows, table)
    core = lax.axis_index("c").astype(jnp.int32).reshape(1)
    towers = tower_call(core, states, next_states, next_slate.T, w_hidden, w_embed)
    own = swap(copies, ("x", "l"))
    other = lax.ppermute(own, "c", pair)
    keep, send, delta = main_call(
        core,
        states,
        towers,
        rewards.reshape(1, sessions),
        slate_ids.T,
        chosen.reshape(1, sessions),
        own,
        other,
        w_embed,
    )

    got = lax.ppermute(send, "c", pair)
    part = (keep + got.astype(F32)).astype(BF16)
    part = in_vmem(plane_kernel, swap(part, XZ), (8, EIGHTH + TOWER, embed))
    part = in_vmem(line_kernel, swap(part, Y), (PLANE, EIGHTH + TOWER, embed))
    pieces = swap(part, XZ)
    other_pieces = lax.ppermute(pieces, "c", pair)

    moment = jax.ShapeDtypeStruct(first_moment.shape, F32)
    scalar = pl.BlockSpec(memory_space=pltpu.SMEM)
    new_first, new_second, direction = pl.pallas_call(
        adam_kernel,
        in_specs=[scalar] + [vmem] * 4,
        out_specs=[vmem] * 3,
        out_shape=[moment, moment, moment],
        compiler_params=PARAMS,
    )(lax.axis_index("x").astype(jnp.int32).reshape(1), rows, pieces, first_moment, second_moment)
    grad_hidden, grad_embed = pl.pallas_call(
        unpack_kernel,
        in_specs=[scalar] + [vmem] * 2,
        out_specs=[vmem] * 2,
        out_shape=[
            jax.ShapeDtypeStruct(w_hidden.shape, F32),
            jax.ShapeDtypeStruct(w_embed.shape, F32),
        ],
        compiler_params=PARAMS,
    )(core, pieces, other_pieces)
    return (new_first, new_second, direction, grad_hidden, grad_embed, delta.reshape(sessions))


def solution(mesh):
    torus = Mesh(mesh.devices.reshape(SIZES), AXES)
    every = P(AXES)
    item = P(ITEM)
    placed = (every,) * 6 + (item,) * 4 + (P(), P())
    return jax.shard_map(
        shards,
        mesh=torus,
        in_specs=placed,
        out_specs=(item, item, item, P(), P(), every),
        check_vma=False,
    )
```

```python
import jax
import jax.numpy as jnp
from jax import lax
from jax.experimental import pallas as pl
from jax.experimental.pallas import tpu as pltpu
from jax.sharding import Mesh
from jax.sharding import PartitionSpec as P

ADAM_STEP = 10
PENALTY = 0.5
DISCOUNT = 0.9
BETA_ONE = 0.9
BETA_TWO = 0.999
EPSILON = 1e-08

AXES = ("h", "z", "x", "l", "c")
SIZES = (4, 8, 4, 2, 2)
ITEM = ("x", "l", "c")
CHIPS = 8
CORES = 2
BLOCK = 256
PACK = 352
DP = (4, 8)
SHARE = BLOCK // 8
PIECE = SHARE + 16
SLATE = 10
F32 = jnp.float32
BF16 = jnp.bfloat16
NT = (((1,), (1,)), ((), ()))
NN = (((1,), (0,)), ((), ()))
PARAMS = pltpu.CompilerParams(vmem_limit_bytes=48 * 1024 * 1024)


def dot(left, right, dims=NN):
    return lax.dot_general(left, right, dims, preferred_element_type=F32)


def copies_kernel(rows_ref, out_ref):
    rows = rows_ref[...].astype(BF16)
    for copy in range(out_ref.shape[0]):
        out_ref[copy] = rows


def tower_kernel(
    core_ref,
    states_ref,
    next_ref,
    upcoming_ref,
    w_hidden_ref,
    w_embed_ref,
    hidden_t_ref,
    users_t_ref,
    next_users_ref,
    low_ref,
    high_ref,
):
    sessions = states_ref.shape[0]
    w_hidden = w_hidden_ref[...]
    w_embed = w_embed_ref[...]
    hidden_t = jnp.maximum(dot(w_hidden.T, states_ref[...], NT), 0.0).astype(BF16)
    hidden_t_ref[...] = hidden_t
    users_t_ref[...] = dot(w_embed.T, hidden_t).astype(BF16)
    next_hidden = jnp.maximum(dot(next_ref[...], w_hidden), 0.0).astype(BF16)
    next_users_ref[...] = dot(next_hidden, w_embed).astype(BF16)

    upcoming = jnp.bitwise_xor(upcoming_ref[...], core_ref[0] * BLOCK)
    padded = jnp.concatenate(
        [upcoming, jnp.zeros((128 - SLATE, sessions), jnp.int32)], axis=0
    )
    for part in range(sessions // 128):
        rows = slice(part * 128, part * 128 + 128)
        turned = padded[:, rows].astype(F32).T.astype(jnp.int32)
        low_ref[rows, :] = jnp.bitwise_and(turned, 127)
        high_ref[rows, :] = lax.shift_right_logical(turned, 7)


def main_kernel(
    core_ref,
    states_ref,
    hidden_t_ref,
    users_t_ref,
    next_users_ref,
    low_ref,
    high_ref,
    rewards_ref,
    slate_ref,
    chosen_ref,
    own_ref,
    other_ref,
    w_embed_ref,
    keep_ref,
    send_ref,
    delta_ref,
    scores_ref,
    next_scores_ref,
    next_q_ref,
    grad_ref,
    grad_hidden_ref,
    grad_embed_ref,
):
    core = core_ref[0]
    sessions = states_ref.shape[0]
    slabs = (own_ref, other_ref)
    outs = (keep_ref, send_ref)
    w_embed = w_embed_ref[...]

    slate = jnp.bitwise_xor(slate_ref[...], core * BLOCK)
    place = lax.broadcasted_iota(jnp.int32, slate.shape, 0)
    clicked = jnp.sum(jnp.where(place == chosen_ref[...], slate, 0), axis=0, keepdims=True)
    sub = lax.broadcasted_iota(jnp.int32, (8, sessions), 0)
    behind = jnp.broadcast_to(clicked, (8, sessions)) - sub

    blocks = [(chip, side) for chip in range(CHIPS) for side in range(CORES)]
    next_users = next_users_ref[...]
    for block, (chip, side) in enumerate(blocks):
        next_scores = dot(next_users, slabs[side][chip], NT)
        next_scores_ref[block * 2] = next_scores[:, :128]
        next_scores_ref[block * 2 + 1] = next_scores[:, 128:]

    highest = jnp.full((8, sessions), -jnp.inf, F32)
    picked = jnp.zeros((8, sessions), F32)
    groups = sessions // 8 // len(blocks)
    for block, (chip, side) in enumerate(blocks):
        for group in range(block * groups, (block + 1) * groups):
            rows = slice(group * 8, group * 8 + 8)
            low = low_ref[rows, :]
            high = high_ref[rows, :]
            found = jnp.zeros((8, 128), F32)
            for chunk in range(next_scores_ref.shape[0]):
                piece = jnp.take_along_axis(
                    next_scores_ref[chunk, rows, :], low, axis=1, mode="promise_in_bounds"
                )
                found = jnp.where(high == chunk, piece, found)
            next_q_ref[rows, :] = found
        scores = dot(slabs[side][chip], users_t_ref[...])
        scores_ref[block] = scores
        for step in range(BLOCK // 8):
            piece = scores[step * 8 : step * 8 + 8]
            highest = jnp.maximum(highest, piece)
            picked = jnp.where(behind == block * BLOCK + step * 8, piece, picked)
    highest = jnp.max(highest, axis=0, keepdims=True)
    picked = jnp.sum(picked, axis=0, keepdims=True)

    next_q = jnp.concatenate(
        [next_q_ref[part * 128 : part * 128 + 128, :].T[:16] for part in range(sessions // 128)],
        axis=1,
    )
    shown = lax.broadcasted_iota(jnp.int32, next_q.shape, 0) < SLATE
    top = jnp.max(jnp.where(shown, next_q, -jnp.inf), axis=0, keepdims=True)
    weights = jnp.where(shown, jnp.exp(next_q - top), 0.0)
    mean = jnp.sum(jnp.where(shown, weights * next_q, 0.0), axis=0, keepdims=True) / jnp.sum(
        weights, axis=0, keepdims=True
    )
    delta = picked - (rewards_ref[...] + DISCOUNT * mean)
    delta_ref[...] = delta

    def exponentials(block, total):
        for step in range(BLOCK // 8):
            rows = slice(step * 8, step * 8 + 8)
            piece = jnp.exp(scores_ref[block, rows, :] - highest)
            scores_ref[block, rows, :] = piece
            total = total + piece
        return total

    total = lax.fori_loop(
        0, CHIPS * CORES, exponentials, jnp.zeros((8, sessions), F32), unroll=8
    )
    total = jnp.sum(total, axis=0, keepdims=True)
    scale = 1.0 / sessions
    gain = jnp.broadcast_to((PENALTY * scale) / total, (8, sessions))
    extra = jnp.broadcast_to((delta - PENALTY) * scale, (8, sessions))

    user_grad_t = jnp.zeros((own_ref.shape[2], sessions), F32)
    for block, (chip, side) in enumerate(blocks):
        for step in range(BLOCK // 16):
            pieces = []
            for inner in range(2):
                row = step * 16 + inner * 8
                piece = scores_ref[block, row : row + 8, :] * gain
                pieces.append(
                    piece + jnp.where(behind == block * BLOCK + row, extra, 0.0)
                )
            grad_ref[block, step * 16 : step * 16 + 16, :] = jnp.concatenate(
                pieces, axis=0
            ).astype(BF16)
        grad = grad_ref[block]
        slab = slabs[side][chip]
        user_grad_t = user_grad_t + dot(slab.T, grad)
        outs[side][chip, :BLOCK, :] = dot(grad, users_t_ref[...], NT).astype(outs[side].dtype)
    user_grad_t = user_grad_t.astype(BF16)

    hidden_t = hidden_t_ref[...]
    grad_embed_ref[...] = dot(hidden_t, user_grad_t, NT)
    back = dot(w_embed, user_grad_t)
    pre_grad_t = jnp.where(hidden_t.astype(F32) > 0, back, 0.0).astype(BF16)
    grad_hidden_ref[...] = dot(states_ref[...].T, pre_grad_t, NT)
    for chip in range(CHIPS):
        for side in range(CORES):
            index = chip * CORES + jnp.bitwise_xor(core, side)
            rows = pl.ds(pl.multiple_of(index * 16, 16), 16)
            for quarter in range(4):
                at = BLOCK + quarter * 16
                outs[side][chip, at : at + 16, :] = grad_hidden_ref[
                    rows, quarter * 128 : quarter * 128 + 128
                ].astype(outs[side].dtype)
            rows = pl.ds(pl.multiple_of(index * 32, 32), 32)
            outs[side][chip, BLOCK + 64 :, :] = grad_embed_ref[rows, :].astype(outs[side].dtype)


def cut_kernel(parts_ref, out_ref):
    def total(first, length):
        rows = slice(first, first + length)
        return sum(parts_ref[chip, rows, :].astype(F32) for chip in range(parts_ref.shape[0]))

    for z in range(DP[1]):
        if z < 4:
            tower = total(BLOCK + z * 16, 16)
        else:
            both = total(BLOCK + 64 + (z - 4) // 2 * 16, 16)
            half = both[(z - 4) % 2 * 8 : (z - 4) % 2 * 8 + 8]
            tower = jnp.concatenate([half, jnp.zeros_like(half)], axis=0)
        cands = total(z * SHARE, SHARE).astype(BF16)
        tower = tower.astype(BF16)
        for h in range(DP[0]):
            out_ref[h * DP[1] + z, :SHARE, :] = cands
            out_ref[h * DP[1] + z, SHARE:, :] = tower


def piece_kernel(parts_ref, out_ref):
    total = sum(parts_ref[part].astype(F32) for part in range(parts_ref.shape[0])).astype(BF16)
    for copy in range(out_ref.shape[0]):
        out_ref[copy] = total


def tower_copies_kernel(pieces_ref, out_ref):
    parts = [pieces_ref[z, SHARE:, :] for z in range(4)]
    for z in range(4, 8, 2):
        halves = [pieces_ref[z + more, SHARE:, :].astype(F32)[:8] for more in range(2)]
        parts.append(jnp.concatenate(halves, axis=0).astype(BF16))
    rows = jnp.concatenate(parts, axis=0)
    for copy in range(out_ref.shape[0]):
        out_ref[copy] = rows


def adam_kernel(
    rows_ref,
    pieces_ref,
    first_ref,
    second_ref,
    tower_ref,
    new_first_ref,
    new_second_ref,
    direction_ref,
    grad_hidden_ref,
    grad_embed_ref,
):
    for item in range(CHIPS * CORES):
        for quarter in range(4):
            grad_hidden_ref[item * 16 : item * 16 + 16, quarter * 128 : quarter * 128 + 128] = (
                tower_ref[item, quarter * 16 : quarter * 16 + 16, :].astype(F32)
            )
        grad_embed_ref[item * 32 : item * 32 + 32, :] = tower_ref[item, 64:, :].astype(F32)
    shape = (first_ref.shape[0], BLOCK)
    onehot = lax.broadcasted_iota(jnp.int32, shape, 0) == rows_ref[...]
    grad = jnp.concatenate([pieces_ref[z, :SHARE, :] for z in range(DP[1])], axis=0)
    table_grad = dot(onehot.astype(F32).astype(BF16), grad)
    new_first = BETA_ONE * first_ref[...] + (1.0 - BETA_ONE) * table_grad
    new_second = BETA_TWO * second_ref[...] + (1.0 - BETA_TWO) * table_grad * table_grad
    new_first_ref[...] = new_first
    new_second_ref[...] = new_second
    correct_one = 1.0 - BETA_ONE**ADAM_STEP
    correct_two = 1.0 - BETA_TWO**ADAM_STEP
    direction_ref[...] = new_first / correct_one / (jnp.sqrt(new_second / correct_two) + EPSILON)


def in_vmem(kernel, array, shape):
    vmem = pl.BlockSpec(memory_space=pltpu.VMEM)
    return pl.pallas_call(
        kernel,
        in_specs=[vmem],
        out_specs=vmem,
        out_shape=jax.ShapeDtypeStruct(shape, BF16),
        compiler_params=PARAMS,
    )(array)


def swap(array, axes):
    return lax.all_to_all(array, axes, 0, 0, tiled=True)


def tower_call(core, states, next_states, next_slate_t, w_hidden, w_embed):
    sessions = states.shape[0]
    hidden, embed = w_embed.shape
    vmem = pl.BlockSpec(memory_space=pltpu.VMEM)
    places = jax.ShapeDtypeStruct((sessions, 128), jnp.int32)
    return pl.pallas_call(
        tower_kernel,
        in_specs=[pl.BlockSpec(memory_space=pltpu.SMEM)] + [vmem] * 5,
        out_specs=[vmem] * 5,
        out_shape=[
            jax.ShapeDtypeStruct((hidden, sessions), BF16),
            jax.ShapeDtypeStruct((embed, sessions), BF16),
            jax.ShapeDtypeStruct((sessions, embed), BF16),
            places,
            places,
        ],
        compiler_params=PARAMS,
    )(core, states, next_states, next_slate_t, w_hidden, w_embed)


def main_call(core, states, towers, rewards, slate_t, chosen, own, other, w_embed):
    sessions, features = states.shape
    hidden, embed = w_embed.shape
    vmem = pl.BlockSpec(memory_space=pltpu.VMEM)
    return pl.pallas_call(
        main_kernel,
        in_specs=[pl.BlockSpec(memory_space=pltpu.SMEM)] + [vmem] * 12,
        out_specs=[vmem] * 3,
        out_shape=[
            jax.ShapeDtypeStruct((CHIPS, PACK, embed), F32),
            jax.ShapeDtypeStruct((CHIPS, PACK, embed), BF16),
            jax.ShapeDtypeStruct((1, sessions), F32),
        ],
        scratch_shapes=[
            pltpu.VMEM((CHIPS * CORES, BLOCK, sessions), F32),
            pltpu.VMEM((CHIPS * CORES * 2, sessions, 128), F32),
            pltpu.VMEM((sessions, 128), F32),
            pltpu.VMEM((CHIPS * CORES, BLOCK, sessions), BF16),
            pltpu.VMEM((features, hidden), F32),
            pltpu.VMEM((hidden, embed), F32),
        ],
        compiler_params=PARAMS,
    )(core, states, *towers, rewards, slate_t, chosen, own, other, w_embed)


def shards(
    states,
    next_states,
    rewards,
    slate_ids,
    chosen,
    next_slate,
    table,
    first_moment,
    second_moment,
    cand_rows,
    w_hidden,
    w_embed,
):
    embed = table.shape[1]
    sessions = states.shape[0]
    vmem = pl.BlockSpec(memory_space=pltpu.VMEM)
    rows = cand_rows.reshape(1, BLOCK)
    pair = [(0, 1), (1, 0)]

    local_rows = table.at[cand_rows].get(mode="promise_in_bounds", unique_indices=True)
    copies = in_vmem(copies_kernel, local_rows, (CHIPS, BLOCK, embed))
    core = lax.axis_index("c").astype(jnp.int32).reshape(1)
    towers = tower_call(core, states, next_states, next_slate.T, w_hidden, w_embed)
    own = swap(copies, ("x", "l"))
    other = lax.ppermute(own, "c", pair)
    keep, send, delta = main_call(
        core,
        states,
        towers,
        rewards.reshape(1, sessions),
        slate_ids.T,
        chosen.reshape(1, sessions),
        own,
        other,
        w_embed,
    )

    got = lax.ppermute(send, "c", pair)
    part = (keep + got.astype(F32)).astype(BF16)
    share = in_vmem(cut_kernel, swap(part, ("x", "l")), (DP[0] * DP[1], PIECE, embed))
    share = in_vmem(piece_kernel, swap(share, ("h", "z")), (DP[1], PIECE, embed))
    pieces = swap(share, "z")
    tower = in_vmem(tower_copies_kernel, pieces, (CHIPS * CORES, PACK - BLOCK, embed))
    tower = swap(tower, ITEM)

    moment = jax.ShapeDtypeStruct(first_moment.shape, F32)
    new_first, new_second, direction, grad_hidden, grad_embed = pl.pallas_call(
        adam_kernel,
        in_specs=[vmem] * 5,
        out_specs=[vmem] * 5,
        out_shape=[
            moment,
            moment,
            moment,
            jax.ShapeDtypeStruct(w_hidden.shape, F32),
            jax.ShapeDtypeStruct(w_embed.shape, F32),
        ],
        compiler_params=PARAMS,
    )(rows, pieces, first_moment, second_moment, tower)
    return (new_first, new_second, direction, grad_hidden, grad_embed, delta.reshape(sessions))


def solution(mesh):
    torus = Mesh(mesh.devices.reshape(SIZES), AXES)
    every = P(AXES)
    item = P(ITEM)
    placed = (every,) * 6 + (item,) * 4 + (P(), P())
    return jax.shard_map(
        shards,
        mesh=torus,
        in_specs=placed,
        out_specs=(item, item, item, P(), P(), every),
        check_vma=False,
    )
```

```python
import jax
import jax.numpy as jnp
from jax import lax
from jax.experimental import pallas as pl
from jax.experimental.pallas import tpu as pltpu
from jax.sharding import Mesh
from jax.sharding import PartitionSpec as P

ADAM_STEP = 10
PENALTY = 0.5
DISCOUNT = 0.9
BETA_ONE = 0.9
BETA_TWO = 0.999
EPSILON = 1e-08

AXES = ("h", "z", "x", "l", "c")
SIZES = (4, 8, 4, 2, 2)
ITEM = ("x", "l", "c")
CHIPS = 8
CORES = 2
BLOCK = 256
PACK = 352
DP = (4, 8)
SHARE = BLOCK // 8
PIECE = SHARE + 16
SLATE = 10
STEPS = 4
F32 = jnp.float32
BF16 = jnp.bfloat16
NT = (((1,), (1,)), ((), ()))
NN = (((1,), (0,)), ((), ()))
PARAMS = pltpu.CompilerParams(vmem_limit_bytes=40 * 1024 * 1024)


def dot(left, right, dims=NN):
    return lax.dot_general(left, right, dims, preferred_element_type=F32)


def copies_kernel(rows_ref, out_ref):
    rows = rows_ref[...].astype(BF16)
    for copy in range(out_ref.shape[0]):
        out_ref[copy] = rows


def tower_kernel(
    core_ref,
    states_ref,
    next_ref,
    upcoming_ref,
    slate_ref,
    chosen_ref,
    w_hidden_ref,
    w_embed_ref,
    hidden_t_ref,
    users_t_ref,
    next_users_ref,
    low_ref,
    high_ref,
    clicked_ref,
):
    sessions = states_ref.shape[0]
    w_hidden = w_hidden_ref[...]
    w_embed = w_embed_ref[...]
    hidden_t = jnp.maximum(dot(w_hidden.T, states_ref[...], NT), 0.0).astype(BF16)
    hidden_t_ref[...] = hidden_t
    users_t_ref[...] = dot(w_embed.T, hidden_t).astype(BF16)
    next_hidden = jnp.maximum(dot(next_ref[...], w_hidden), 0.0).astype(BF16)
    next_users_ref[...] = dot(next_hidden, w_embed).astype(BF16)

    slate = jnp.bitwise_xor(slate_ref[...], core_ref[0] * BLOCK)
    place = lax.broadcasted_iota(jnp.int32, slate.shape, 0)
    clicked_ref[...] = jnp.sum(
        jnp.where(place == chosen_ref[...], slate, 0), axis=0, keepdims=True
    )
    upcoming = jnp.bitwise_xor(upcoming_ref[...], core_ref[0] * BLOCK)
    padded = jnp.concatenate(
        [upcoming, jnp.zeros((128 - SLATE, sessions), jnp.int32)], axis=0
    )
    for part in range(sessions // 128):
        rows = slice(part * 128, part * 128 + 128)
        turned = padded[:, rows].astype(F32).T.astype(jnp.int32)
        low_ref[rows, :] = jnp.bitwise_and(turned, 127)
        high_ref[rows, :] = lax.shift_right_logical(turned, 7)


def score_side(
    side,
    slab_ref,
    users_t_ref,
    next_users_ref,
    low_ref,
    high_ref,
    behind,
    highest,
    picked,
    before_ref,
    scores_ref,
    next_scores_ref,
    next_q_ref,
):
    next_users = next_users_ref[...]
    for chip in range(CHIPS):
        next_scores = dot(next_users, slab_ref[chip], NT)
        next_scores_ref[chip * 2] = next_scores[:, :128]
        next_scores_ref[chip * 2 + 1] = next_scores[:, 128:]
    groups = next_users.shape[0] // 8 // CHIPS
    for chip in range(CHIPS):
        for group in range(chip * groups, (chip + 1) * groups):
            rows = slice(group * 8, group * 8 + 8)
            low = low_ref[rows, :]
            high = high_ref[rows, :]
            found = jnp.zeros((8, 128), F32) if before_ref is None else before_ref[rows, :]
            for chunk in range(2 * CHIPS):
                piece = jnp.take_along_axis(
                    next_scores_ref[chunk, rows, :], low, axis=1, mode="promise_in_bounds"
                )
                number = (chunk // 2 * CORES + side) * 2 + chunk % 2
                found = jnp.where(high == number, piece, found)
            next_q_ref[rows, :] = found
        scores = dot(slab_ref[chip], users_t_ref[...])
        scores_ref[chip] = scores
        first = (chip * CORES + side) * BLOCK
        for step in range(BLOCK // 8):
            piece = scores[step * 8 : step * 8 + 8]
            highest = jnp.maximum(highest, piece)
            picked = jnp.where(behind == first + step * 8, piece, picked)
    return highest, picked


def behind_of(clicked_ref):
    sessions = clicked_ref.shape[1]
    sub = lax.broadcasted_iota(jnp.int32, (8, sessions), 0)
    return jnp.broadcast_to(clicked_ref[...], (8, sessions)) - sub


def own_kernel(
    users_t_ref,
    next_users_ref,
    low_ref,
    high_ref,
    clicked_ref,
    own_ref,
    scores_ref,
    highest_ref,
    picked_ref,
    next_q_ref,
    next_scores_ref,
):
    shape = highest_ref.shape
    highest_ref[...], picked_ref[...] = score_side(
        0,
        own_ref,
        users_t_ref,
        next_users_ref,
        low_ref,
        high_ref,
        behind_of(clicked_ref),
        jnp.full(shape, -jnp.inf, F32),
        jnp.zeros(shape, F32),
        None,
        scores_ref,
        next_scores_ref,
        next_q_ref,
    )


def main_kernel(
    core_ref,
    states_ref,
    hidden_t_ref,
    users_t_ref,
    next_users_ref,
    low_ref,
    high_ref,
    clicked_ref,
    rewards_ref,
    own_ref,
    other_ref,
    own_scores_ref,
    own_highest_ref,
    own_picked_ref,
    own_next_q_ref,
    w_embed_ref,
    keep_ref,
    send_ref,
    delta_ref,
    scores_ref,
    next_scores_ref,
    next_q_ref,
    grad_ref,
    grad_hidden_ref,
    grad_embed_ref,
):
    core = core_ref[0]
    sessions = states_ref.shape[0]
    slabs = (own_ref, other_ref)
    outs = (keep_ref, send_ref)
    w_embed = w_embed_ref[...]
    blocks = [(chip, side) for chip in range(CHIPS) for side in range(CORES)]
    behind = behind_of(clicked_ref)
    highest, picked = score_side(
        1,
        other_ref,
        users_t_ref,
        next_users_ref,
        low_ref,
        high_ref,
        behind,
        own_highest_ref[...],
        own_picked_ref[...],
        own_next_q_ref,
        scores_ref.at[1],
        next_scores_ref,
        next_q_ref,
    )
    highest = jnp.max(highest, axis=0, keepdims=True)
    picked = jnp.sum(picked, axis=0, keepdims=True)

    next_q = jnp.concatenate(
        [next_q_ref[part * 128 : part * 128 + 128, :].T[:16] for part in range(sessions // 128)],
        axis=1,
    )
    shown = lax.broadcasted_iota(jnp.int32, next_q.shape, 0) < SLATE
    top = jnp.max(jnp.where(shown, next_q, -jnp.inf), axis=0, keepdims=True)
    weights = jnp.where(shown, jnp.exp(next_q - top), 0.0)
    mean = jnp.sum(jnp.where(shown, weights * next_q, 0.0), axis=0, keepdims=True) / jnp.sum(
        weights, axis=0, keepdims=True
    )
    delta = picked - (rewards_ref[...] + DISCOUNT * mean)
    delta_ref[...] = delta

    total = jnp.zeros((8, sessions), F32)
    for side, from_ref in enumerate((own_scores_ref, scores_ref.at[1])):

        def exponentials(chip, total):
            for step in range(BLOCK // 8):
                rows = slice(step * 8, step * 8 + 8)
                piece = jnp.exp(from_ref[chip, rows, :] - highest)
                scores_ref[side, chip, rows, :] = piece
                total = total + piece
            return total

        total = lax.fori_loop(0, CHIPS, exponentials, total, unroll=4)
    total = jnp.sum(total, axis=0, keepdims=True)
    scale = 1.0 / sessions
    gain = jnp.broadcast_to((PENALTY * scale) / total, (8, sessions))
    extra = jnp.broadcast_to((delta - PENALTY) * scale, (8, sessions))

    user_grad_t = jnp.zeros((own_ref.shape[2], sessions), F32)
    for block, (chip, side) in enumerate(blocks):
        for step in range(BLOCK // 16):
            pieces = []
            for inner in range(2):
                row = step * 16 + inner * 8
                piece = scores_ref[side, chip, row : row + 8, :] * gain
                pieces.append(
                    piece + jnp.where(behind == block * BLOCK + row, extra, 0.0)
                )
            grad_ref[block, step * 16 : step * 16 + 16, :] = jnp.concatenate(
                pieces, axis=0
            ).astype(BF16)
        grad = grad_ref[block]
        slab = slabs[side][chip]
        user_grad_t = user_grad_t + dot(slab.T, grad)
        outs[side][chip, :BLOCK, :] = dot(grad, users_t_ref[...], NT).astype(outs[side].dtype)
    user_grad_t = user_grad_t.astype(BF16)

    hidden_t = hidden_t_ref[...]
    grad_embed_ref[...] = dot(hidden_t, user_grad_t, NT)
    back = dot(w_embed, user_grad_t)
    pre_grad_t = jnp.where(hidden_t.astype(F32) > 0, back, 0.0).astype(BF16)
    grad_hidden_ref[...] = dot(states_ref[...].T, pre_grad_t, NT)
    for chip in range(CHIPS):
        for side in range(CORES):
            index = chip * CORES + jnp.bitwise_xor(core, side)
            rows = pl.ds(pl.multiple_of(index * 16, 16), 16)
            for quarter in range(4):
                at = BLOCK + quarter * 16
                outs[side][chip, at : at + 16, :] = grad_hidden_ref[
                    rows, quarter * 128 : quarter * 128 + 128
                ].astype(outs[side].dtype)
            rows = pl.ds(pl.multiple_of(index * 32, 32), 32)
            outs[side][chip, BLOCK + 64 :, :] = grad_embed_ref[rows, :].astype(outs[side].dtype)


def cut_kernel(parts_ref, out_ref):
    def total(first, length):
        rows = slice(first, first + length)
        return sum(parts_ref[chip, rows, :].astype(F32) for chip in range(parts_ref.shape[0]))

    for z in range(DP[1]):
        if z < 4:
            tower = total(BLOCK + z * 16, 16)
        else:
            both = total(BLOCK + 64 + (z - 4) // 2 * 16, 16)
            half = both[(z - 4) % 2 * 8 : (z - 4) % 2 * 8 + 8]
            tower = jnp.concatenate([half, jnp.zeros_like(half)], axis=0)
        cands = total(z * SHARE, SHARE).astype(BF16)
        tower = tower.astype(BF16)
        for h in range(DP[0]):
            out_ref[h * DP[1] + z, :SHARE, :] = cands
            out_ref[h * DP[1] + z, SHARE:, :] = tower


def piece_kernel(parts_ref, out_ref):
    total = sum(parts_ref[part].astype(F32) for part in range(parts_ref.shape[0])).astype(BF16)
    for copy in range(out_ref.shape[0]):
        out_ref[copy] = total


def tower_copies_kernel(pieces_ref, out_ref):
    parts = [pieces_ref[z, SHARE:, :] for z in range(4)]
    for z in range(4, 8, 2):
        halves = [pieces_ref[z + more, SHARE:, :].astype(F32)[:8] for more in range(2)]
        parts.append(jnp.concatenate(halves, axis=0).astype(BF16))
    rows = jnp.concatenate(parts, axis=0)
    for copy in range(out_ref.shape[0]):
        out_ref[copy] = rows


def adam_kernel(
    rows_ref,
    pieces_ref,
    first_ref,
    second_ref,
    tower_ref,
    new_first_out,
    new_second_out,
    direction_out,
    grad_hidden_out,
    grad_embed_out,
    new_first_ref,
    new_second_ref,
    direction_ref,
    grad_hidden_ref,
    grad_embed_ref,
    sems,
):
    copies = []

    def send(source, target):
        copies.append(pltpu.make_async_copy(source, target, sems.at[len(copies)]))
        copies[-1].start()

    for item in range(CHIPS * CORES):
        for quarter in range(4):
            grad_hidden_ref[item * 16 : item * 16 + 16, quarter * 128 : quarter * 128 + 128] = (
                tower_ref[item, quarter * 16 : quarter * 16 + 16, :].astype(F32)
            )
        grad_embed_ref[item * 32 : item * 32 + 32, :] = tower_ref[item, 64:, :].astype(F32)
    send(grad_hidden_ref, grad_hidden_out)
    send(grad_embed_ref, grad_embed_out)
    grad = jnp.concatenate([pieces_ref[z, :SHARE, :] for z in range(DP[1])], axis=0)
    length = first_ref.shape[0] // STEPS
    correct_one = 1.0 - BETA_ONE**ADAM_STEP
    correct_two = 1.0 - BETA_TWO**ADAM_STEP
    for step in range(STEPS):
        rows = pl.ds(step * length, length)
        place = lax.broadcasted_iota(jnp.int32, (length, BLOCK), 0) + step * length
        onehot = place == rows_ref[...]
        table_grad = dot(onehot.astype(F32).astype(BF16), grad)
        new_first = BETA_ONE * first_ref[rows, :] + (1.0 - BETA_ONE) * table_grad
        new_second = BETA_TWO * second_ref[rows, :] + (1.0 - BETA_TWO) * table_grad * table_grad
        new_first_ref[rows, :] = new_first
        new_second_ref[rows, :] = new_second
        direction_ref[rows, :] = (
            new_first / correct_one / (jnp.sqrt(new_second / correct_two) + EPSILON)
        )
        send(new_first_ref.at[rows], new_first_out.at[rows])
        send(new_second_ref.at[rows], new_second_out.at[rows])
        send(direction_ref.at[rows], direction_out.at[rows])
    for copy in copies:
        copy.wait()


def in_vmem(kernel, array, shape):
    vmem = pl.BlockSpec(memory_space=pltpu.VMEM)
    return pl.pallas_call(
        kernel,
        in_specs=[vmem],
        out_specs=vmem,
        out_shape=jax.ShapeDtypeStruct(shape, BF16),
        compiler_params=PARAMS,
    )(array)


def swap(array, axes):
    return lax.all_to_all(array, axes, 0, 0, tiled=True)


def tower_call(core, states, next_states, next_slate_t, slate_t, chosen, w_hidden, w_embed):
    sessions = states.shape[0]
    hidden, embed = w_embed.shape
    vmem = pl.BlockSpec(memory_space=pltpu.VMEM)
    places = jax.ShapeDtypeStruct((sessions, 128), jnp.int32)
    return pl.pallas_call(
        tower_kernel,
        in_specs=[pl.BlockSpec(memory_space=pltpu.SMEM)] + [vmem] * 7,
        out_specs=[vmem] * 6,
        out_shape=[
            jax.ShapeDtypeStruct((hidden, sessions), BF16),
            jax.ShapeDtypeStruct((embed, sessions), BF16),
            jax.ShapeDtypeStruct((sessions, embed), BF16),
            places,
            places,
            jax.ShapeDtypeStruct((1, sessions), jnp.int32),
        ],
        compiler_params=PARAMS,
    )(core, states, next_states, next_slate_t, slate_t, chosen, w_hidden, w_embed)


def own_call(towers, own):
    sessions = towers[1].shape[1]
    vmem = pl.BlockSpec(memory_space=pltpu.VMEM)
    line = jax.ShapeDtypeStruct((8, sessions), F32)
    return pl.pallas_call(
        own_kernel,
        in_specs=[vmem] * 6,
        out_specs=[vmem] * 4,
        out_shape=[
            jax.ShapeDtypeStruct((CHIPS, BLOCK, sessions), F32),
            line,
            line,
            jax.ShapeDtypeStruct((sessions, 128), F32),
        ],
        scratch_shapes=[pltpu.VMEM((CHIPS * 2, sessions, 128), F32)],
        compiler_params=PARAMS,
    )(*towers[1:], own)


def main_call(core, states, towers, rewards, own, other, begun, w_embed):
    sessions, features = states.shape
    hidden, embed = w_embed.shape
    vmem = pl.BlockSpec(memory_space=pltpu.VMEM)
    pack = (CHIPS, PACK, embed)
    return pl.pallas_call(
        main_kernel,
        in_specs=[pl.BlockSpec(memory_space=pltpu.SMEM)] + [vmem] * 15,
        out_specs=[vmem] * 3,
        out_shape=[
            jax.ShapeDtypeStruct(pack, F32),
            jax.ShapeDtypeStruct(pack, BF16),
            jax.ShapeDtypeStruct((1, sessions), F32),
        ],
        scratch_shapes=[
            pltpu.VMEM((CORES, CHIPS, BLOCK, sessions), F32),
            pltpu.VMEM((CHIPS * 2, sessions, 128), F32),
            pltpu.VMEM((sessions, 128), F32),
            pltpu.VMEM((CHIPS * CORES, BLOCK, sessions), BF16),
            pltpu.VMEM((features, hidden), F32),
            pltpu.VMEM((hidden, embed), F32),
        ],
        compiler_params=PARAMS,
    )(core, states, *towers, rewards, own, other, *begun, w_embed)


def shards(
    states,
    next_states,
    rewards,
    slate_ids,
    chosen,
    next_slate,
    table,
    first_moment,
    second_moment,
    cand_rows,
    w_hidden,
    w_embed,
):
    embed = table.shape[1]
    sessions = states.shape[0]
    vmem = pl.BlockSpec(memory_space=pltpu.VMEM)
    rows = cand_rows.reshape(1, BLOCK)
    pair = [(0, 1), (1, 0)]

    local_rows = table.at[cand_rows].get(mode="promise_in_bounds", unique_indices=True)
    copies = in_vmem(copies_kernel, local_rows, (CHIPS, BLOCK, embed))
    core = lax.axis_index("c").astype(jnp.int32).reshape(1)
    chosen = chosen.reshape(1, sessions)
    towers = tower_call(
        core, states, next_states, next_slate.T, slate_ids.T, chosen, w_hidden, w_embed
    )
    own = swap(copies, ("x", "l"))
    other = lax.ppermute(own, "c", pair)
    begun = own_call(towers, own)
    rewards = rewards.reshape(1, sessions)
    keep, send, delta = main_call(core, states, towers, rewards, own, other, begun, w_embed)

    got = lax.ppermute(send, "c", pair)
    part = (keep + got.astype(F32)).astype(BF16)
    share = in_vmem(cut_kernel, swap(part, ("x", "l")), (DP[0] * DP[1], PIECE, embed))
    share = in_vmem(piece_kernel, swap(share, ("h", "z")), (DP[1], PIECE, embed))
    pieces = swap(share, "z")
    tower = in_vmem(tower_copies_kernel, pieces, (CHIPS * CORES, PACK - BLOCK, embed))
    tower = swap(tower, ITEM)

    last = [jax.ShapeDtypeStruct(first_moment.shape, F32)] * 3
    last += [jax.ShapeDtypeStruct(array.shape, F32) for array in (w_hidden, w_embed)]
    new_first, new_second, direction, grad_hidden, grad_embed = pl.pallas_call(
        adam_kernel,
        in_specs=[vmem] * 5,
        out_specs=[pl.BlockSpec(memory_space=pl.ANY)] * 5,
        out_shape=last,
        scratch_shapes=[pltpu.VMEM(out.shape, F32) for out in last]
        + [pltpu.SemaphoreType.DMA((2 + 3 * STEPS,))],
        compiler_params=PARAMS,
    )(rows, pieces, first_moment, second_moment, tower)
    return (new_first, new_second, direction, grad_hidden, grad_embed, delta.reshape(sessions))


def solution(mesh):
    torus = Mesh(mesh.devices.reshape(SIZES), AXES)
    every = P(AXES)
    item = P(ITEM)
    placed = (every,) * 6 + (item,) * 4 + (P(), P())
    return jax.shard_map(
        shards,
        mesh=torus,
        in_specs=placed,
        out_specs=(item, item, item, P(), P(), every),
        check_vma=False,
    )
```

```python
import jax
import jax.numpy as jnp
from jax import lax
from jax.experimental import pallas as pl
from jax.experimental.pallas import tpu as pltpu
from jax.sharding import Mesh
from jax.sharding import PartitionSpec as P

ADAM_STEP = 10
PENALTY = 0.5
DISCOUNT = 0.9
BETA_ONE = 0.9
BETA_TWO = 0.999
EPSILON = 1e-08

AXES = ("h", "z", "x", "l", "c")
SIZES = (4, 8, 4, 2, 2)
ITEM = ("x", "l", "c")
CHIPS = 8
CORES = 2
BLOCK = 256
PACK = 352
DP = 32
PIECE = 16
TOWER_PIECES = (PACK - BLOCK) // 8
SLATE = 10
STEPS = 4
F32 = jnp.float32
BF16 = jnp.bfloat16
NT = (((1,), (1,)), ((), ()))
NN = (((1,), (0,)), ((), ()))
PARAMS = pltpu.CompilerParams(vmem_limit_bytes=40 * 1024 * 1024)


def dot(left, right, dims=NN):
    return lax.dot_general(left, right, dims, preferred_element_type=F32)


def copies_kernel(rows_ref, out_ref):
    rows = rows_ref[...].astype(BF16)
    for copy in range(out_ref.shape[0]):
        out_ref[copy] = rows


def tower_kernel(
    core_ref,
    states_ref,
    next_ref,
    upcoming_ref,
    slate_ref,
    chosen_ref,
    w_hidden_ref,
    w_embed_ref,
    hidden_t_ref,
    users_t_ref,
    next_users_ref,
    low_ref,
    high_ref,
    clicked_ref,
):
    sessions = states_ref.shape[0]
    w_hidden = w_hidden_ref[...]
    w_embed = w_embed_ref[...]
    hidden_t = jnp.maximum(dot(w_hidden.T, states_ref[...], NT), 0.0).astype(BF16)
    hidden_t_ref[...] = hidden_t
    users_t_ref[...] = dot(w_embed.T, hidden_t).astype(BF16)
    next_hidden = jnp.maximum(dot(next_ref[...], w_hidden), 0.0).astype(BF16)
    next_users_ref[...] = dot(next_hidden, w_embed).astype(BF16)

    slate = jnp.bitwise_xor(slate_ref[...], core_ref[0] * BLOCK)
    place = lax.broadcasted_iota(jnp.int32, slate.shape, 0)
    clicked_ref[...] = jnp.sum(
        jnp.where(place == chosen_ref[...], slate, 0), axis=0, keepdims=True
    )
    upcoming = jnp.bitwise_xor(upcoming_ref[...], core_ref[0] * BLOCK)
    padded = jnp.concatenate(
        [upcoming, jnp.zeros((128 - SLATE, sessions), jnp.int32)], axis=0
    )
    for part in range(sessions // 128):
        rows = slice(part * 128, part * 128 + 128)
        turned = padded[:, rows].astype(F32).T.astype(jnp.int32)
        low_ref[rows, :] = jnp.bitwise_and(turned, 127)
        high_ref[rows, :] = lax.shift_right_logical(turned, 7)


def score_side(
    side,
    slab_ref,
    users_t_ref,
    next_users_ref,
    low_ref,
    high_ref,
    behind,
    highest,
    picked,
    before_ref,
    scores_ref,
    next_scores_ref,
    next_q_ref,
):
    next_users = next_users_ref[...]
    for chip in range(CHIPS):
        next_scores = dot(next_users, slab_ref[chip], NT)
        next_scores_ref[chip * 2] = next_scores[:, :128]
        next_scores_ref[chip * 2 + 1] = next_scores[:, 128:]
    groups = next_users.shape[0] // 8 // CHIPS
    for chip in range(CHIPS):
        for group in range(chip * groups, (chip + 1) * groups):
            rows = slice(group * 8, group * 8 + 8)
            low = low_ref[rows, :]
            high = high_ref[rows, :]
            found = jnp.zeros((8, 128), F32) if before_ref is None else before_ref[rows, :]
            for chunk in range(2 * CHIPS):
                piece = jnp.take_along_axis(
                    next_scores_ref[chunk, rows, :], low, axis=1, mode="promise_in_bounds"
                )
                number = (chunk // 2 * CORES + side) * 2 + chunk % 2
                found = jnp.where(high == number, piece, found)
            next_q_ref[rows, :] = found
        scores = dot(slab_ref[chip], users_t_ref[...])
        scores_ref[chip] = scores
        first = (chip * CORES + side) * BLOCK
        for step in range(BLOCK // 8):
            piece = scores[step * 8 : step * 8 + 8]
            highest = jnp.maximum(highest, piece)
            picked = jnp.where(behind == first + step * 8, piece, picked)
    return highest, picked


def behind_of(clicked_ref):
    sessions = clicked_ref.shape[1]
    sub = lax.broadcasted_iota(jnp.int32, (8, sessions), 0)
    return jnp.broadcast_to(clicked_ref[...], (8, sessions)) - sub


def own_kernel(
    users_t_ref,
    next_users_ref,
    low_ref,
    high_ref,
    clicked_ref,
    own_ref,
    scores_ref,
    highest_ref,
    picked_ref,
    next_q_ref,
    next_scores_ref,
):
    shape = highest_ref.shape
    highest_ref[...], picked_ref[...] = score_side(
        0,
        own_ref,
        users_t_ref,
        next_users_ref,
        low_ref,
        high_ref,
        behind_of(clicked_ref),
        jnp.full(shape, -jnp.inf, F32),
        jnp.zeros(shape, F32),
        None,
        scores_ref,
        next_scores_ref,
        next_q_ref,
    )


def main_kernel(
    core_ref,
    states_ref,
    hidden_t_ref,
    users_t_ref,
    next_users_ref,
    low_ref,
    high_ref,
    clicked_ref,
    rewards_ref,
    own_ref,
    other_ref,
    own_scores_ref,
    own_highest_ref,
    own_picked_ref,
    own_next_q_ref,
    w_embed_ref,
    keep_ref,
    send_ref,
    delta_ref,
    scores_ref,
    next_scores_ref,
    next_q_ref,
    grad_ref,
    grad_hidden_ref,
    grad_embed_ref,
):
    core = core_ref[0]
    sessions = states_ref.shape[0]
    slabs = (own_ref, other_ref)
    outs = (keep_ref, send_ref)
    w_embed = w_embed_ref[...]
    blocks = [(chip, side) for chip in range(CHIPS) for side in range(CORES)]
    behind = behind_of(clicked_ref)
    highest, picked = score_side(
        1,
        other_ref,
        users_t_ref,
        next_users_ref,
        low_ref,
        high_ref,
        behind,
        own_highest_ref[...],
        own_picked_ref[...],
        own_next_q_ref,
        scores_ref.at[1],
        next_scores_ref,
        next_q_ref,
    )
    highest = jnp.max(highest, axis=0, keepdims=True)
    picked = jnp.sum(picked, axis=0, keepdims=True)

    next_q = jnp.concatenate(
        [next_q_ref[part * 128 : part * 128 + 128, :].T[:16] for part in range(sessions // 128)],
        axis=1,
    )
    shown = lax.broadcasted_iota(jnp.int32, next_q.shape, 0) < SLATE
    top = jnp.max(jnp.where(shown, next_q, -jnp.inf), axis=0, keepdims=True)
    weights = jnp.where(shown, jnp.exp(next_q - top), 0.0)
    mean = jnp.sum(jnp.where(shown, weights * next_q, 0.0), axis=0, keepdims=True) / jnp.sum(
        weights, axis=0, keepdims=True
    )
    delta = picked - (rewards_ref[...] + DISCOUNT * mean)
    delta_ref[...] = delta

    total = jnp.zeros((8, sessions), F32)
    for side, from_ref in enumerate((own_scores_ref, scores_ref.at[1])):

        def exponentials(chip, total):
            for step in range(BLOCK // 8):
                rows = slice(step * 8, step * 8 + 8)
                piece = jnp.exp(from_ref[chip, rows, :] - highest)
                scores_ref[side, chip, rows, :] = piece
                total = total + piece
            return total

        total = lax.fori_loop(0, CHIPS, exponentials, total, unroll=4)
    total = jnp.sum(total, axis=0, keepdims=True)
    scale = 1.0 / sessions
    gain = jnp.broadcast_to((PENALTY * scale) / total, (8, sessions))
    extra = jnp.broadcast_to((delta - PENALTY) * scale, (8, sessions))

    user_grad_t = jnp.zeros((own_ref.shape[2], sessions), F32)
    for block, (chip, side) in enumerate(blocks):
        for step in range(BLOCK // 16):
            pieces = []
            for inner in range(2):
                row = step * 16 + inner * 8
                piece = scores_ref[side, chip, row : row + 8, :] * gain
                pieces.append(
                    piece + jnp.where(behind == block * BLOCK + row, extra, 0.0)
                )
            grad_ref[block, step * 16 : step * 16 + 16, :] = jnp.concatenate(
                pieces, axis=0
            ).astype(BF16)
        grad = grad_ref[block]
        slab = slabs[side][chip]
        user_grad_t = user_grad_t + dot(slab.T, grad)
        outs[side][chip, :BLOCK, :] = dot(grad, users_t_ref[...], NT).astype(outs[side].dtype)
    user_grad_t = user_grad_t.astype(BF16)

    hidden_t = hidden_t_ref[...]
    grad_embed_ref[...] = dot(hidden_t, user_grad_t, NT)
    back = dot(w_embed, user_grad_t)
    pre_grad_t = jnp.where(hidden_t.astype(F32) > 0, back, 0.0).astype(BF16)
    grad_hidden_ref[...] = dot(states_ref[...].T, pre_grad_t, NT)
    for chip in range(CHIPS):
        for side in range(CORES):
            index = chip * CORES + jnp.bitwise_xor(core, side)
            rows = pl.ds(pl.multiple_of(index * 16, 16), 16)
            for quarter in range(4):
                at = BLOCK + quarter * 16
                outs[side][chip, at : at + 16, :] = grad_hidden_ref[
                    rows, quarter * 128 : quarter * 128 + 128
                ].astype(outs[side].dtype)
            rows = pl.ds(pl.multiple_of(index * 32, 32), 32)
            outs[side][chip, BLOCK + 64 :, :] = grad_embed_ref[rows, :].astype(outs[side].dtype)


def cut_kernel(parts_ref, out_ref):
    def total(first):
        rows = slice(first, first + 16)
        return sum(parts_ref[chip, rows, :].astype(F32) for chip in range(parts_ref.shape[0]))

    towers = []
    for first in range(BLOCK, PACK, 16):
        both = total(first)
        towers += [both[:8], both[8:]]
    for first in range(0, BLOCK, 16):
        both = total(first)
        for inner in range(2):
            piece = first // 8 + inner
            tower = towers[piece] if piece < TOWER_PIECES else jnp.zeros_like(both[:8])
            out_ref[piece] = jnp.concatenate(
                [both[inner * 8 : inner * 8 + 8], tower], axis=0
            ).astype(BF16)


def piece_kernel(parts_ref, out_ref):
    total = sum(parts_ref[part].astype(F32) for part in range(parts_ref.shape[0])).astype(BF16)
    for copy in range(out_ref.shape[0]):
        out_ref[copy] = total


def tower_copies_kernel(pieces_ref, out_ref):
    rows = jnp.concatenate(
        [pieces_ref[piece].astype(F32)[8:] for piece in range(TOWER_PIECES)], axis=0
    ).astype(BF16)
    for copy in range(out_ref.shape[0]):
        out_ref[copy] = rows


def adam_kernel(
    rows_ref,
    pieces_ref,
    first_ref,
    second_ref,
    tower_ref,
    new_first_out,
    new_second_out,
    direction_out,
    grad_hidden_out,
    grad_embed_out,
    new_first_ref,
    new_second_ref,
    direction_ref,
    grad_hidden_ref,
    grad_embed_ref,
    sems,
):
    copies = []

    def send(source, target):
        copies.append(pltpu.make_async_copy(source, target, sems.at[len(copies)]))
        copies[-1].start()

    for sender in range(CHIPS * CORES):
        item = sender // 4 * 4 + sender % 2 * 2 + sender // 2 % 2
        for quarter in range(4):
            grad_hidden_ref[item * 16 : item * 16 + 16, quarter * 128 : quarter * 128 + 128] = (
                tower_ref[sender, quarter * 16 : quarter * 16 + 16, :].astype(F32)
            )
        grad_embed_ref[item * 32 : item * 32 + 32, :] = tower_ref[sender, 64:, :].astype(F32)
    send(grad_hidden_ref, grad_hidden_out)
    send(grad_embed_ref, grad_embed_out)
    grad = jnp.concatenate(
        [pieces_ref[piece].astype(F32)[:8] for piece in range(DP)], axis=0
    ).astype(BF16)
    length = first_ref.shape[0] // STEPS
    correct_one = 1.0 - BETA_ONE**ADAM_STEP
    correct_two = 1.0 - BETA_TWO**ADAM_STEP
    for step in range(STEPS):
        rows = pl.ds(step * length, length)
        place = lax.broadcasted_iota(jnp.int32, (length, BLOCK), 0) + step * length
        onehot = place == rows_ref[...]
        table_grad = dot(onehot.astype(F32).astype(BF16), grad)
        new_first = BETA_ONE * first_ref[rows, :] + (1.0 - BETA_ONE) * table_grad
        new_second = BETA_TWO * second_ref[rows, :] + (1.0 - BETA_TWO) * table_grad * table_grad
        new_first_ref[rows, :] = new_first
        new_second_ref[rows, :] = new_second
        direction_ref[rows, :] = (
            new_first / correct_one / (jnp.sqrt(new_second / correct_two) + EPSILON)
        )
        send(new_first_ref.at[rows], new_first_out.at[rows])
        send(new_second_ref.at[rows], new_second_out.at[rows])
        send(direction_ref.at[rows], direction_out.at[rows])
    for copy in copies:
        copy.wait()


def in_vmem(kernel, array, shape):
    vmem = pl.BlockSpec(memory_space=pltpu.VMEM)
    return pl.pallas_call(
        kernel,
        in_specs=[vmem],
        out_specs=vmem,
        out_shape=jax.ShapeDtypeStruct(shape, BF16),
        compiler_params=PARAMS,
    )(array)


def swap(array, axes):
    return lax.all_to_all(array, axes, 0, 0, tiled=True)


def tower_call(core, states, next_states, next_slate_t, slate_t, chosen, w_hidden, w_embed):
    sessions = states.shape[0]
    hidden, embed = w_embed.shape
    vmem = pl.BlockSpec(memory_space=pltpu.VMEM)
    places = jax.ShapeDtypeStruct((sessions, 128), jnp.int32)
    return pl.pallas_call(
        tower_kernel,
        in_specs=[pl.BlockSpec(memory_space=pltpu.SMEM)] + [vmem] * 7,
        out_specs=[vmem] * 6,
        out_shape=[
            jax.ShapeDtypeStruct((hidden, sessions), BF16),
            jax.ShapeDtypeStruct((embed, sessions), BF16),
            jax.ShapeDtypeStruct((sessions, embed), BF16),
            places,
            places,
            jax.ShapeDtypeStruct((1, sessions), jnp.int32),
        ],
        compiler_params=PARAMS,
    )(core, states, next_states, next_slate_t, slate_t, chosen, w_hidden, w_embed)


def own_call(towers, own):
    sessions = towers[1].shape[1]
    vmem = pl.BlockSpec(memory_space=pltpu.VMEM)
    line = jax.ShapeDtypeStruct((8, sessions), F32)
    return pl.pallas_call(
        own_kernel,
        in_specs=[vmem] * 6,
        out_specs=[vmem] * 4,
        out_shape=[
            jax.ShapeDtypeStruct((CHIPS, BLOCK, sessions), F32),
            line,
            line,
            jax.ShapeDtypeStruct((sessions, 128), F32),
        ],
        scratch_shapes=[pltpu.VMEM((CHIPS * 2, sessions, 128), F32)],
        compiler_params=PARAMS,
    )(*towers[1:], own)


def main_call(core, states, towers, rewards, own, other, begun, w_embed):
    sessions, features = states.shape
    hidden, embed = w_embed.shape
    vmem = pl.BlockSpec(memory_space=pltpu.VMEM)
    pack = (CHIPS, PACK, embed)
    return pl.pallas_call(
        main_kernel,
        in_specs=[pl.BlockSpec(memory_space=pltpu.SMEM)] + [vmem] * 15,
        out_specs=[vmem] * 3,
        out_shape=[
            jax.ShapeDtypeStruct(pack, F32),
            jax.ShapeDtypeStruct(pack, BF16),
            jax.ShapeDtypeStruct((1, sessions), F32),
        ],
        scratch_shapes=[
            pltpu.VMEM((CORES, CHIPS, BLOCK, sessions), F32),
            pltpu.VMEM((CHIPS * 2, sessions, 128), F32),
            pltpu.VMEM((sessions, 128), F32),
            pltpu.VMEM((CHIPS * CORES, BLOCK, sessions), BF16),
            pltpu.VMEM((features, hidden), F32),
            pltpu.VMEM((hidden, embed), F32),
        ],
        compiler_params=PARAMS,
    )(core, states, *towers, rewards, own, other, *begun, w_embed)


def shards(
    states,
    next_states,
    rewards,
    slate_ids,
    chosen,
    next_slate,
    table,
    first_moment,
    second_moment,
    cand_rows,
    w_hidden,
    w_embed,
):
    embed = table.shape[1]
    sessions = states.shape[0]
    vmem = pl.BlockSpec(memory_space=pltpu.VMEM)
    rows = cand_rows.reshape(1, BLOCK)
    pair = [(0, 1), (1, 0)]

    local_rows = table.at[cand_rows].get(mode="promise_in_bounds", unique_indices=True)
    copies = in_vmem(copies_kernel, local_rows, (CHIPS, BLOCK, embed))
    core = lax.axis_index("c").astype(jnp.int32).reshape(1)
    chosen = chosen.reshape(1, sessions)
    towers = tower_call(
        core, states, next_states, next_slate.T, slate_ids.T, chosen, w_hidden, w_embed
    )
    own = swap(copies, ("x", "l"))
    other = lax.ppermute(own, "c", pair)
    begun = own_call(towers, own)
    rewards = rewards.reshape(1, sessions)
    keep, send, delta = main_call(core, states, towers, rewards, own, other, begun, w_embed)

    got = lax.ppermute(send, "c", pair)
    part = (keep + got.astype(F32)).astype(BF16)
    pieces = in_vmem(cut_kernel, swap(part, ("x", "l")), (DP, PIECE, embed))
    pieces = in_vmem(piece_kernel, swap(pieces, ("z", "h")), (DP, PIECE, embed))
    pieces = swap(pieces, ("z", "h"))
    tower = in_vmem(tower_copies_kernel, pieces, (CHIPS * CORES, PACK - BLOCK, embed))
    tower = swap(tower, ("x", "c", "l"))

    last = [jax.ShapeDtypeStruct(first_moment.shape, F32)] * 3
    last += [jax.ShapeDtypeStruct(array.shape, F32) for array in (w_hidden, w_embed)]
    new_first, new_second, direction, grad_hidden, grad_embed = pl.pallas_call(
        adam_kernel,
        in_specs=[vmem] * 5,
        out_specs=[pl.BlockSpec(memory_space=pl.ANY)] * 5,
        out_shape=last,
        scratch_shapes=[pltpu.VMEM(out.shape, F32) for out in last]
        + [pltpu.SemaphoreType.DMA((2 + 3 * STEPS,))],
        compiler_params=PARAMS,
    )(rows, pieces, first_moment, second_moment, tower)
    return (new_first, new_second, direction, grad_hidden, grad_embed, delta.reshape(sessions))


def solution(mesh):
    torus = Mesh(mesh.devices.reshape(SIZES), AXES)
    every = P(AXES)
    item = P(ITEM)
    placed = (every,) * 6 + (item,) * 4 + (P(), P())
    return jax.shard_map(
        shards,
        mesh=torus,
        in_specs=placed,
        out_specs=(item, item, item, P(), P(), every),
        check_vma=False,
    )
```

```python
import jax
import jax.numpy as jnp
from jax import lax
from jax.experimental import pallas as pl
from jax.experimental.pallas import tpu as pltpu
from jax.sharding import Mesh
from jax.sharding import PartitionSpec as P

ADAM_STEP = 10
PENALTY = 0.5
DISCOUNT = 0.9
BETA_ONE = 0.9
BETA_TWO = 0.999
EPSILON = 1e-08

AXES = ("h", "z", "x", "l", "c")
SIZES = (4, 8, 4, 2, 2)
ITEM = ("x", "l", "c")
CHIPS = 8
CORES = 2
BLOCK = 256
PACK = 352
DP = 32
PIECE = 16
TOWER_PIECES = (PACK - BLOCK) // 8
SLATE = 10
STEPS = 4
F32 = jnp.float32
BF16 = jnp.bfloat16
NT = (((1,), (1,)), ((), ()))
NN = (((1,), (0,)), ((), ()))
PARAMS = pltpu.CompilerParams(vmem_limit_bytes=40 * 1024 * 1024)


def dot(left, right, dims=NN):
    return lax.dot_general(left, right, dims, preferred_element_type=F32)


def copies_kernel(rows_ref, out_ref):
    rows = rows_ref[...].astype(BF16)
    for copy in range(out_ref.shape[0]):
        out_ref[copy] = rows


def tower_kernel(
    core_ref,
    states_ref,
    next_ref,
    upcoming_ref,
    slate_ref,
    chosen_ref,
    w_hidden_ref,
    w_embed_ref,
    hidden_t_ref,
    users_t_ref,
    next_users_ref,
    low_ref,
    high_ref,
    clicked_ref,
):
    sessions = states_ref.shape[0]
    w_hidden = w_hidden_ref[...]
    w_embed = w_embed_ref[...]
    hidden_t = jnp.maximum(dot(w_hidden.T, states_ref[...], NT), 0.0).astype(BF16)
    hidden_t_ref[...] = hidden_t
    users_t_ref[...] = dot(w_embed.T, hidden_t).astype(BF16)
    next_hidden = jnp.maximum(dot(next_ref[...], w_hidden), 0.0).astype(BF16)
    next_users_ref[...] = dot(next_hidden, w_embed).astype(BF16)

    slate = jnp.bitwise_xor(slate_ref[...], core_ref[0] * BLOCK)
    place = lax.broadcasted_iota(jnp.int32, slate.shape, 0)
    clicked_ref[...] = jnp.sum(
        jnp.where(place == chosen_ref[...], slate, 0), axis=0, keepdims=True
    )
    upcoming = jnp.bitwise_xor(upcoming_ref[...], core_ref[0] * BLOCK)
    padded = jnp.concatenate(
        [upcoming, jnp.zeros((128 - SLATE, sessions), jnp.int32)], axis=0
    )
    for part in range(sessions // 128):
        rows = slice(part * 128, part * 128 + 128)
        turned = padded[:, rows].astype(F32).T.astype(jnp.int32)
        low_ref[rows, :] = jnp.bitwise_and(turned, 127)
        high_ref[rows, :] = lax.shift_right_logical(turned, 7)


def score_side(
    side,
    slab_ref,
    users_t_ref,
    next_users_ref,
    low_ref,
    high_ref,
    behind,
    highest,
    picked,
    before_ref,
    scores_ref,
    next_scores_ref,
    next_q_ref,
):
    next_users = next_users_ref[...]
    for chip in range(CHIPS):
        next_scores = dot(next_users, slab_ref[chip], NT)
        next_scores_ref[chip * 2] = next_scores[:, :128]
        next_scores_ref[chip * 2 + 1] = next_scores[:, 128:]
    groups = next_users.shape[0] // 8 // CHIPS
    for chip in range(CHIPS):
        for group in range(chip * groups, (chip + 1) * groups):
            rows = slice(group * 8, group * 8 + 8)
            low = low_ref[rows, :]
            high = high_ref[rows, :]
            found = jnp.zeros((8, 128), F32) if before_ref is None else before_ref[rows, :]
            for chunk in range(2 * CHIPS):
                piece = jnp.take_along_axis(
                    next_scores_ref[chunk, rows, :], low, axis=1, mode="promise_in_bounds"
                )
                number = (chunk // 2 * CORES + side) * 2 + chunk % 2
                found = jnp.where(high == number, piece, found)
            next_q_ref[rows, :] = found
        scores = dot(slab_ref[chip], users_t_ref[...])
        scores_ref[chip] = scores
        first = (chip * CORES + side) * BLOCK
        for step in range(BLOCK // 8):
            piece = scores[step * 8 : step * 8 + 8]
            highest = jnp.maximum(highest, piece)
            picked = jnp.where(behind == first + step * 8, piece, picked)
    return highest, picked


def behind_of(clicked_ref):
    sessions = clicked_ref.shape[1]
    sub = lax.broadcasted_iota(jnp.int32, (8, sessions), 0)
    return jnp.broadcast_to(clicked_ref[...], (8, sessions)) - sub


def own_kernel(
    users_t_ref,
    next_users_ref,
    low_ref,
    high_ref,
    clicked_ref,
    own_ref,
    scores_ref,
    highest_ref,
    picked_ref,
    next_q_ref,
    next_scores_ref,
):
    shape = highest_ref.shape
    highest_ref[...], picked_ref[...] = score_side(
        0,
        own_ref,
        users_t_ref,
        next_users_ref,
        low_ref,
        high_ref,
        behind_of(clicked_ref),
        jnp.full(shape, -jnp.inf, F32),
        jnp.zeros(shape, F32),
        None,
        scores_ref,
        next_scores_ref,
        next_q_ref,
    )


def main_kernel(
    core_ref,
    states_ref,
    hidden_t_ref,
    users_t_ref,
    next_users_ref,
    low_ref,
    high_ref,
    clicked_ref,
    rewards_ref,
    own_ref,
    other_ref,
    own_scores_ref,
    own_highest_ref,
    own_picked_ref,
    own_next_q_ref,
    w_embed_ref,
    send_ref,
    delta_ref,
    own_grad_ref,
    user_grad_ref,
    pre_grad_ref,
    scores_ref,
    next_scores_ref,
    next_q_ref,
    other_grad_ref,
):
    sessions = states_ref.shape[0]
    slabs = (own_ref, other_ref)
    grads = (own_grad_ref, other_grad_ref)
    w_embed = w_embed_ref[...]
    blocks = [(chip, side) for chip in range(CHIPS) for side in range(CORES)]
    behind = behind_of(clicked_ref)
    highest, picked = score_side(
        1,
        other_ref,
        users_t_ref,
        next_users_ref,
        low_ref,
        high_ref,
        behind,
        own_highest_ref[...],
        own_picked_ref[...],
        own_next_q_ref,
        scores_ref.at[1],
        next_scores_ref,
        next_q_ref,
    )
    highest = jnp.max(highest, axis=0, keepdims=True)
    picked = jnp.sum(picked, axis=0, keepdims=True)

    next_q = jnp.concatenate(
        [next_q_ref[part * 128 : part * 128 + 128, :].T[:16] for part in range(sessions // 128)],
        axis=1,
    )
    shown = lax.broadcasted_iota(jnp.int32, next_q.shape, 0) < SLATE
    top = jnp.max(jnp.where(shown, next_q, -jnp.inf), axis=0, keepdims=True)
    weights = jnp.where(shown, jnp.exp(next_q - top), 0.0)
    mean = jnp.sum(jnp.where(shown, weights * next_q, 0.0), axis=0, keepdims=True) / jnp.sum(
        weights, axis=0, keepdims=True
    )
    delta = picked - (rewards_ref[...] + DISCOUNT * mean)
    delta_ref[...] = delta

    total = jnp.zeros((8, sessions), F32)
    for side, from_ref in enumerate((own_scores_ref, scores_ref.at[1])):

        def exponentials(chip, total):
            for step in range(BLOCK // 8):
                rows = slice(step * 8, step * 8 + 8)
                piece = jnp.exp(from_ref[chip, rows, :] - highest)
                scores_ref[side, chip, rows, :] = piece
                total = total + piece
            return total

        total = lax.fori_loop(0, CHIPS, exponentials, total, unroll=4)
    total = jnp.sum(total, axis=0, keepdims=True)
    scale = 1.0 / sessions
    gain = jnp.broadcast_to((PENALTY * scale) / total, (8, sessions))
    extra = jnp.broadcast_to((delta - PENALTY) * scale, (8, sessions))

    user_grad_t = jnp.zeros((own_ref.shape[2], sessions), F32)
    for block, (chip, side) in enumerate(blocks):
        for step in range(BLOCK // 16):
            pieces = []
            for inner in range(2):
                row = step * 16 + inner * 8
                piece = scores_ref[side, chip, row : row + 8, :] * gain
                pieces.append(
                    piece + jnp.where(behind == block * BLOCK + row, extra, 0.0)
                )
            grads[side][chip, step * 16 : step * 16 + 16, :] = jnp.concatenate(
                pieces, axis=0
            ).astype(BF16)
        grad = grads[side][chip]
        user_grad_t = user_grad_t + dot(slabs[side][chip].T, grad)
        if side == 1:
            send_ref[chip, :BLOCK, :] = dot(grad, users_t_ref[...], NT).astype(BF16)
    user_grad_t = user_grad_t.astype(BF16)
    user_grad_ref[...] = user_grad_t
    hidden_t = hidden_t_ref[...]
    back = dot(w_embed, user_grad_t)
    pre_grad_t = jnp.where(hidden_t.astype(F32) > 0, back, 0.0).astype(BF16)
    pre_grad_ref[...] = pre_grad_t
    tower_half(1 - core_ref[0], states_ref, hidden_t_ref, user_grad_t, pre_grad_t, send_ref)


def tower_half(half, states_ref, hidden_t_ref, user_grad_t, pre_grad_t, out_ref):
    lanes = pl.ds(pl.multiple_of(half * 128, 128), 128)
    grad_hidden = dot(states_ref[:, lanes].T, pre_grad_t, NT).astype(out_ref.dtype)
    rows = pl.ds(pl.multiple_of(half * 256, 256), 256)
    grad_embed = dot(hidden_t_ref[rows, :], user_grad_t, NT).astype(out_ref.dtype)
    for chip in range(CHIPS):
        for quarter in range(4):
            at = BLOCK + quarter * 16
            out_ref[chip, at : at + 16, :] = grad_hidden[
                chip * 16 : chip * 16 + 16, quarter * 128 : quarter * 128 + 128
            ]
        out_ref[chip, BLOCK + 64 :, :] = grad_embed[chip * 32 : chip * 32 + 32]


def keep_kernel(
    core_ref, states_ref, hidden_t_ref, users_t_ref, grad_ref, user_grad_ref, pre_grad_ref, keep_ref
):
    for chip in range(CHIPS):
        keep_ref[chip, :BLOCK, :] = dot(grad_ref[chip], users_t_ref[...], NT)
    tower_half(
        core_ref[0], states_ref, hidden_t_ref, user_grad_ref[...], pre_grad_ref[...], keep_ref
    )


def cut_kernel(parts_ref, out_ref):
    def total(first):
        rows = slice(first, first + 16)
        return sum(parts_ref[chip, rows, :].astype(F32) for chip in range(parts_ref.shape[0]))

    towers = []
    for first in range(BLOCK, PACK, 16):
        both = total(first)
        towers += [both[:8], both[8:]]
    for first in range(0, BLOCK, 16):
        both = total(first)
        for inner in range(2):
            piece = first // 8 + inner
            tower = towers[piece] if piece < TOWER_PIECES else jnp.zeros_like(both[:8])
            out_ref[piece] = jnp.concatenate(
                [both[inner * 8 : inner * 8 + 8], tower], axis=0
            ).astype(BF16)


def piece_kernel(parts_ref, out_ref):
    total = sum(parts_ref[part].astype(F32) for part in range(parts_ref.shape[0])).astype(BF16)
    for copy in range(out_ref.shape[0]):
        out_ref[copy] = total


def tower_copies_kernel(pieces_ref, out_ref):
    rows = jnp.concatenate(
        [pieces_ref[piece].astype(F32)[8:] for piece in range(TOWER_PIECES)], axis=0
    ).astype(BF16)
    for copy in range(out_ref.shape[0]):
        out_ref[copy] = rows


def adam_kernel(
    rows_ref,
    pieces_ref,
    first_ref,
    second_ref,
    tower_ref,
    new_first_out,
    new_second_out,
    direction_out,
    grad_hidden_out,
    grad_embed_out,
    new_first_ref,
    new_second_ref,
    direction_ref,
    grad_hidden_ref,
    grad_embed_ref,
    sems,
):
    copies = []

    def send(source, target):
        copies.append(pltpu.make_async_copy(source, target, sems.at[len(copies)]))
        copies[-1].start()

    for sender in range(CHIPS * CORES):
        half, chip = sender // 2 % 2, sender // 4 * 2 + sender % 2
        row = half * 128 + chip * 16
        for quarter in range(4):
            grad_hidden_ref[row : row + 16, quarter * 128 : quarter * 128 + 128] = tower_ref[
                sender, quarter * 16 : quarter * 16 + 16, :
            ].astype(F32)
        row = half * 256 + chip * 32
        grad_embed_ref[row : row + 32, :] = tower_ref[sender, 64:, :].astype(F32)
    send(grad_hidden_ref, grad_hidden_out)
    send(grad_embed_ref, grad_embed_out)
    grad = jnp.concatenate(
        [pieces_ref[piece].astype(F32)[:8] for piece in range(DP)], axis=0
    ).astype(BF16)
    length = first_ref.shape[0] // STEPS
    correct_one = 1.0 - BETA_ONE**ADAM_STEP
    correct_two = 1.0 - BETA_TWO**ADAM_STEP
    for step in range(STEPS):
        rows = pl.ds(step * length, length)
        place = lax.broadcasted_iota(jnp.int32, (length, BLOCK), 0) + step * length
        onehot = place == rows_ref[...]
        table_grad = dot(onehot.astype(F32).astype(BF16), grad)
        new_first = BETA_ONE * first_ref[rows, :] + (1.0 - BETA_ONE) * table_grad
        new_second = BETA_TWO * second_ref[rows, :] + (1.0 - BETA_TWO) * table_grad * table_grad
        new_first_ref[rows, :] = new_first
        new_second_ref[rows, :] = new_second
        direction_ref[rows, :] = (
            new_first / correct_one / (jnp.sqrt(new_second / correct_two) + EPSILON)
        )
        send(new_first_ref.at[rows], new_first_out.at[rows])
        send(new_second_ref.at[rows], new_second_out.at[rows])
        send(direction_ref.at[rows], direction_out.at[rows])
    for copy in copies:
        copy.wait()


def in_vmem(kernel, array, shape):
    vmem = pl.BlockSpec(memory_space=pltpu.VMEM)
    return pl.pallas_call(
        kernel,
        in_specs=[vmem],
        out_specs=vmem,
        out_shape=jax.ShapeDtypeStruct(shape, BF16),
        compiler_params=PARAMS,
    )(array)


def swap(array, axes):
    return lax.all_to_all(array, axes, 0, 0, tiled=True)


def tower_call(core, states, next_states, next_slate_t, slate_t, chosen, w_hidden, w_embed):
    sessions = states.shape[0]
    hidden, embed = w_embed.shape
    vmem = pl.BlockSpec(memory_space=pltpu.VMEM)
    places = jax.ShapeDtypeStruct((sessions, 128), jnp.int32)
    return pl.pallas_call(
        tower_kernel,
        in_specs=[pl.BlockSpec(memory_space=pltpu.SMEM)] + [vmem] * 7,
        out_specs=[vmem] * 6,
        out_shape=[
            jax.ShapeDtypeStruct((hidden, sessions), BF16),
            jax.ShapeDtypeStruct((embed, sessions), BF16),
            jax.ShapeDtypeStruct((sessions, embed), BF16),
            places,
            places,
            jax.ShapeDtypeStruct((1, sessions), jnp.int32),
        ],
        compiler_params=PARAMS,
    )(core, states, next_states, next_slate_t, slate_t, chosen, w_hidden, w_embed)


def own_call(towers, own):
    sessions = towers[1].shape[1]
    vmem = pl.BlockSpec(memory_space=pltpu.VMEM)
    line = jax.ShapeDtypeStruct((8, sessions), F32)
    return pl.pallas_call(
        own_kernel,
        in_specs=[vmem] * 6,
        out_specs=[vmem] * 4,
        out_shape=[
            jax.ShapeDtypeStruct((CHIPS, BLOCK, sessions), F32),
            line,
            line,
            jax.ShapeDtypeStruct((sessions, 128), F32),
        ],
        scratch_shapes=[pltpu.VMEM((CHIPS * 2, sessions, 128), F32)],
        compiler_params=PARAMS,
    )(*towers[1:], own)


def main_call(core, states, towers, rewards, own, other, begun, w_embed):
    sessions = states.shape[0]
    hidden, embed = w_embed.shape
    vmem = pl.BlockSpec(memory_space=pltpu.VMEM)
    scalar = pl.BlockSpec(memory_space=pltpu.SMEM)
    send, delta, *rest = pl.pallas_call(
        main_kernel,
        in_specs=[scalar] + [vmem] * 15,
        out_specs=[vmem] * 5,
        out_shape=[
            jax.ShapeDtypeStruct((CHIPS, PACK, embed), BF16),
            jax.ShapeDtypeStruct((1, sessions), F32),
            jax.ShapeDtypeStruct((CHIPS, BLOCK, sessions), BF16),
            jax.ShapeDtypeStruct((embed, sessions), BF16),
            jax.ShapeDtypeStruct((hidden, sessions), BF16),
        ],
        scratch_shapes=[
            pltpu.VMEM((CORES, CHIPS, BLOCK, sessions), F32),
            pltpu.VMEM((CHIPS * 2, sessions, 128), F32),
            pltpu.VMEM((sessions, 128), F32),
            pltpu.VMEM((CHIPS, BLOCK, sessions), BF16),
        ],
        compiler_params=PARAMS,
    )(core, states, *towers, rewards, own, other, *begun, w_embed)
    keep = pl.pallas_call(
        keep_kernel,
        in_specs=[scalar] + [vmem] * 6,
        out_specs=vmem,
        out_shape=jax.ShapeDtypeStruct((CHIPS, PACK, embed), F32),
        compiler_params=PARAMS,
    )(core, states, *towers[:2], *rest)
    return keep, send, delta


def shards(
    states,
    next_states,
    rewards,
    slate_ids,
    chosen,
    next_slate,
    table,
    first_moment,
    second_moment,
    cand_rows,
    w_hidden,
    w_embed,
):
    embed = table.shape[1]
    sessions = states.shape[0]
    vmem = pl.BlockSpec(memory_space=pltpu.VMEM)
    rows = cand_rows.reshape(1, BLOCK)
    pair = [(0, 1), (1, 0)]

    local_rows = table.at[cand_rows].get(mode="promise_in_bounds", unique_indices=True)
    copies = in_vmem(copies_kernel, local_rows, (CHIPS, BLOCK, embed))
    core = lax.axis_index("c").astype(jnp.int32).reshape(1)
    chosen = chosen.reshape(1, sessions)
    towers = tower_call(
        core, states, next_states, next_slate.T, slate_ids.T, chosen, w_hidden, w_embed
    )
    own = swap(copies, ("x", "l"))
    other = lax.ppermute(own, "c", pair)
    begun = own_call(towers, own)
    rewards = rewards.reshape(1, sessions)
    keep, send, delta = main_call(core, states, towers, rewards, own, other, begun, w_embed)

    got = lax.ppermute(send, "c", pair)
    part = (keep + got.astype(F32)).astype(BF16)
    pieces = in_vmem(cut_kernel, swap(part, ("x", "l")), (DP, PIECE, embed))
    pieces = in_vmem(piece_kernel, swap(pieces, ("z", "h")), (DP, PIECE, embed))
    pieces = swap(pieces, ("z", "h"))
    tower = in_vmem(tower_copies_kernel, pieces, (CHIPS * CORES, PACK - BLOCK, embed))
    tower = swap(tower, ("x", "c", "l"))

    last = [jax.ShapeDtypeStruct(first_moment.shape, F32)] * 3
    last += [jax.ShapeDtypeStruct(array.shape, F32) for array in (w_hidden, w_embed)]
    new_first, new_second, direction, grad_hidden, grad_embed = pl.pallas_call(
        adam_kernel,
        in_specs=[vmem] * 5,
        out_specs=[pl.BlockSpec(memory_space=pl.ANY)] * 5,
        out_shape=last,
        scratch_shapes=[pltpu.VMEM(out.shape, F32) for out in last]
        + [pltpu.SemaphoreType.DMA((2 + 3 * STEPS,))],
        compiler_params=PARAMS,
    )(rows, pieces, first_moment, second_moment, tower)
    return (new_first, new_second, direction, grad_hidden, grad_embed, delta.reshape(sessions))


def solution(mesh):
    torus = Mesh(mesh.devices.reshape(SIZES), AXES)
    every = P(AXES)
    item = P(ITEM)
    placed = (every,) * 6 + (item,) * 4 + (P(), P())
    return jax.shard_map(
        shards,
        mesh=torus,
        in_specs=placed,
        out_specs=(item, item, item, P(), P(), every),
        check_vma=False,
    )
```

```python
import jax
import jax.numpy as jnp
from jax import lax
from jax.experimental import pallas as pl
from jax.experimental.pallas import tpu as pltpu
from jax.sharding import Mesh
from jax.sharding import PartitionSpec as P

ADAM_STEP = 10
PENALTY = 0.5
DISCOUNT = 0.9
BETA_ONE = 0.9
BETA_TWO = 0.999
EPSILON = 1e-08

AXES = ("h", "z", "x", "l", "c")
SIZES = (4, 8, 4, 2, 2)
ITEM = ("x", "l", "c")
CHIPS = 8
CORES = 2
BLOCK = 256
PACK = 352
DP = 32
PIECE = 16
TOWER_PIECES = (PACK - BLOCK) // 8
SLATE = 10
STEPS = 4
F32 = jnp.float32
BF16 = jnp.bfloat16
NT = (((1,), (1,)), ((), ()))
NN = (((1,), (0,)), ((), ()))
PARAMS = pltpu.CompilerParams(vmem_limit_bytes=40 * 1024 * 1024)


def dot(left, right, dims=NN):
    return lax.dot_general(left, right, dims, preferred_element_type=F32)


def copies_kernel(rows_ref, out_ref):
    rows = rows_ref[...].astype(BF16)
    for copy in range(out_ref.shape[0]):
        out_ref[copy] = rows


def tower_kernel(
    core_ref,
    states_ref,
    next_ref,
    upcoming_ref,
    slate_ref,
    chosen_ref,
    w_hidden_ref,
    w_embed_ref,
    hidden_t_ref,
    users_t_ref,
    next_users_ref,
    low_ref,
    high_ref,
    clicked_ref,
):
    sessions = states_ref.shape[0]
    w_hidden = w_hidden_ref[...]
    w_embed = w_embed_ref[...]
    hidden_t = jnp.maximum(dot(w_hidden.T, states_ref[...], NT), 0.0).astype(BF16)
    hidden_t_ref[...] = hidden_t
    users_t_ref[...] = dot(w_embed.T, hidden_t).astype(BF16)
    next_hidden = jnp.maximum(dot(next_ref[...], w_hidden), 0.0).astype(BF16)
    next_users_ref[...] = dot(next_hidden, w_embed).astype(BF16)

    slate = jnp.bitwise_xor(slate_ref[...], core_ref[0] * BLOCK)
    place = lax.broadcasted_iota(jnp.int32, slate.shape, 0)
    clicked_ref[...] = jnp.sum(
        jnp.where(place == chosen_ref[...], slate, 0), axis=0, keepdims=True
    )
    upcoming = jnp.bitwise_xor(upcoming_ref[...], core_ref[0] * BLOCK)
    padded = jnp.concatenate(
        [upcoming, jnp.zeros((128 - SLATE, sessions), jnp.int32)], axis=0
    )
    for part in range(sessions // 128):
        rows = slice(part * 128, part * 128 + 128)
        turned = padded[:, rows].astype(F32).T.astype(jnp.int32)
        low_ref[rows, :] = jnp.bitwise_and(turned, 127)
        high_ref[rows, :] = lax.shift_right_logical(turned, 7)


def score_side(
    side,
    slab_ref,
    users_t_ref,
    next_users_ref,
    low_ref,
    high_ref,
    behind,
    highest,
    picked,
    before_ref,
    scores_ref,
    next_scores_ref,
    next_q_ref,
):
    next_users = next_users_ref[...]
    for chip in range(CHIPS):
        next_scores = dot(next_users, slab_ref[chip], NT)
        next_scores_ref[chip * 2] = next_scores[:, :128]
        next_scores_ref[chip * 2 + 1] = next_scores[:, 128:]
    groups = next_users.shape[0] // 8 // CHIPS
    for chip in range(CHIPS):
        for group in range(chip * groups, (chip + 1) * groups):
            rows = slice(group * 8, group * 8 + 8)
            low = low_ref[rows, :]
            high = high_ref[rows, :]
            found = jnp.zeros((8, 128), F32) if before_ref is None else before_ref[rows, :]
            for chunk in range(2 * CHIPS):
                piece = jnp.take_along_axis(
                    next_scores_ref[chunk, rows, :], low, axis=1, mode="promise_in_bounds"
                )
                number = (chunk // 2 * CORES + side) * 2 + chunk % 2
                found = jnp.where(high == number, piece, found)
            next_q_ref[rows, :] = found
        scores = dot(slab_ref[chip], users_t_ref[...])
        scores_ref[chip] = scores
        first = (chip * CORES + side) * BLOCK
        for step in range(BLOCK // 8):
            piece = scores[step * 8 : step * 8 + 8]
            highest = jnp.maximum(highest, piece)
            picked = jnp.where(behind == first + step * 8, piece, picked)
    return highest, picked


def behind_of(clicked_ref):
    sessions = clicked_ref.shape[1]
    sub = lax.broadcasted_iota(jnp.int32, (8, sessions), 0)
    return jnp.broadcast_to(clicked_ref[...], (8, sessions)) - sub


def own_kernel(
    users_t_ref,
    next_users_ref,
    low_ref,
    high_ref,
    clicked_ref,
    own_ref,
    scores_ref,
    highest_ref,
    picked_ref,
    next_q_ref,
    next_scores_ref,
):
    shape = highest_ref.shape
    highest_ref[...], picked_ref[...] = score_side(
        0,
        own_ref,
        users_t_ref,
        next_users_ref,
        low_ref,
        high_ref,
        behind_of(clicked_ref),
        jnp.full(shape, -jnp.inf, F32),
        jnp.zeros(shape, F32),
        None,
        scores_ref,
        next_scores_ref,
        next_q_ref,
    )


def main_kernel(
    core_ref,
    states_ref,
    hidden_t_ref,
    users_t_ref,
    next_users_ref,
    low_ref,
    high_ref,
    clicked_ref,
    rewards_ref,
    own_ref,
    other_ref,
    own_scores_ref,
    own_highest_ref,
    own_picked_ref,
    own_next_q_ref,
    w_embed_ref,
    send_ref,
    delta_ref,
    own_grad_ref,
    user_grad_ref,
    pre_grad_ref,
    scores_ref,
    next_scores_ref,
    next_q_ref,
    other_grad_ref,
):
    sessions = states_ref.shape[0]
    slabs = (own_ref, other_ref)
    grads = (own_grad_ref, other_grad_ref)
    w_embed = w_embed_ref[...]
    blocks = [(chip, side) for chip in range(CHIPS) for side in range(CORES)]
    behind = behind_of(clicked_ref)
    highest, picked = score_side(
        1,
        other_ref,
        users_t_ref,
        next_users_ref,
        low_ref,
        high_ref,
        behind,
        own_highest_ref[...],
        own_picked_ref[...],
        own_next_q_ref,
        scores_ref.at[1],
        next_scores_ref,
        next_q_ref,
    )
    highest = jnp.max(highest, axis=0, keepdims=True)
    picked = jnp.sum(picked, axis=0, keepdims=True)

    next_q = jnp.concatenate(
        [next_q_ref[part * 128 : part * 128 + 128, :].T[:16] for part in range(sessions // 128)],
        axis=1,
    )
    shown = lax.broadcasted_iota(jnp.int32, next_q.shape, 0) < SLATE
    top = jnp.max(jnp.where(shown, next_q, -jnp.inf), axis=0, keepdims=True)
    weights = jnp.where(shown, jnp.exp(next_q - top), 0.0)
    mean = jnp.sum(jnp.where(shown, weights * next_q, 0.0), axis=0, keepdims=True) / jnp.sum(
        weights, axis=0, keepdims=True
    )
    delta = picked - (rewards_ref[...] + DISCOUNT * mean)
    delta_ref[...] = delta

    total = jnp.zeros((8, sessions), F32)
    for side, from_ref in enumerate((own_scores_ref, scores_ref.at[1])):

        def exponentials(chip, total):
            for step in range(BLOCK // 8):
                rows = slice(step * 8, step * 8 + 8)
                piece = jnp.exp(from_ref[chip, rows, :] - highest)
                scores_ref[side, chip, rows, :] = piece
                total = total + piece
            return total

        total = lax.fori_loop(0, CHIPS, exponentials, total, unroll=4)
    total = jnp.sum(total, axis=0, keepdims=True)
    scale = 1.0 / sessions
    gain = jnp.broadcast_to((PENALTY * scale) / total, (8, sessions))
    extra = jnp.broadcast_to((delta - PENALTY) * scale, (8, sessions))

    user_grad_t = jnp.zeros((own_ref.shape[2], sessions), F32)
    for block, (chip, side) in enumerate(blocks):
        for step in range(BLOCK // 16):
            pieces = []
            for inner in range(2):
                row = step * 16 + inner * 8
                piece = scores_ref[side, chip, row : row + 8, :] * gain
                pieces.append(
                    piece + jnp.where(behind == block * BLOCK + row, extra, 0.0)
                )
            grads[side][chip, step * 16 : step * 16 + 16, :] = jnp.concatenate(
                pieces, axis=0
            ).astype(BF16)
        grad = grads[side][chip]
        user_grad_t = user_grad_t + dot(slabs[side][chip].T, grad)
        if side == 1:
            send_ref[chip, :BLOCK, :] = dot(grad, users_t_ref[...], NT).astype(BF16)
    user_grad_t = user_grad_t.astype(BF16)
    user_grad_ref[...] = user_grad_t
    hidden_t = hidden_t_ref[...]
    back = dot(w_embed, user_grad_t)
    pre_grad_t = jnp.where(hidden_t.astype(F32) > 0, back, 0.0).astype(BF16)
    pre_grad_ref[...] = pre_grad_t
    tower_half(1 - core_ref[0], states_ref, hidden_t_ref, user_grad_t, pre_grad_t, send_ref)


def tower_half(half, states_ref, hidden_t_ref, user_grad_t, pre_grad_t, out_ref):
    lanes = pl.ds(pl.multiple_of(half * 128, 128), 128)
    grad_hidden = dot(states_ref[:, lanes].T, pre_grad_t, NT).astype(out_ref.dtype)
    rows = pl.ds(pl.multiple_of(half * 256, 256), 256)
    grad_embed = dot(hidden_t_ref[rows, :], user_grad_t, NT).astype(out_ref.dtype)
    for chip in range(CHIPS):
        for quarter in range(4):
            at = BLOCK + quarter * 16
            out_ref[chip, at : at + 16, :] = grad_hidden[
                chip * 16 : chip * 16 + 16, quarter * 128 : quarter * 128 + 128
            ]
        out_ref[chip, BLOCK + 64 :, :] = grad_embed[chip * 32 : chip * 32 + 32]


def keep_kernel(
    core_ref, states_ref, hidden_t_ref, users_t_ref, grad_ref, user_grad_ref, pre_grad_ref, keep_ref
):
    for chip in range(CHIPS):
        keep_ref[chip, :BLOCK, :] = dot(grad_ref[chip], users_t_ref[...], NT)
    tower_half(
        core_ref[0], states_ref, hidden_t_ref, user_grad_ref[...], pre_grad_ref[...], keep_ref
    )


def cut_kernel(parts_ref, out_ref):
    def total(first):
        rows = slice(first, first + 16)
        return sum(parts_ref[chip, rows, :].astype(F32) for chip in range(parts_ref.shape[0]))

    towers = []
    for first in range(BLOCK, PACK, 16):
        both = total(first)
        towers += [both[:8], both[8:]]
    for first in range(0, BLOCK, 16):
        both = total(first)
        for inner in range(2):
            piece = first // 8 + inner
            tower = towers[piece] if piece < TOWER_PIECES else jnp.zeros_like(both[:8])
            out_ref[piece] = jnp.concatenate(
                [both[inner * 8 : inner * 8 + 8], tower], axis=0
            ).astype(BF16)


def piece_kernel(parts_ref, out_ref):
    total = sum(parts_ref[part].astype(F32) for part in range(parts_ref.shape[0])).astype(BF16)
    for copy in range(out_ref.shape[0]):
        out_ref[copy] = total


def tower_copies_kernel(pieces_ref, out_ref):
    rows = jnp.concatenate(
        [pieces_ref[piece].astype(F32)[8:] for piece in range(TOWER_PIECES)], axis=0
    ).astype(BF16)
    for copy in range(out_ref.shape[0]):
        out_ref[copy] = rows


def adam_kernel(
    rows_ref,
    pieces_ref,
    first_ref,
    second_ref,
    tower_ref,
    new_first_out,
    new_second_out,
    direction_out,
    grad_hidden_out,
    grad_embed_out,
    new_first_ref,
    new_second_ref,
    direction_ref,
    grad_hidden_ref,
    grad_embed_ref,
    sems,
):
    copies = []

    def send(source, target):
        copies.append(pltpu.make_async_copy(source, target, sems.at[len(copies)]))
        copies[-1].start()

    for sender in range(CHIPS * CORES):
        half, chip = sender // 2 % 2, sender // 4 * 2 + sender % 2
        row = half * 128 + chip * 16
        for quarter in range(4):
            grad_hidden_ref[row : row + 16, quarter * 128 : quarter * 128 + 128] = tower_ref[
                sender, quarter * 16 : quarter * 16 + 16, :
            ].astype(F32)
        row = half * 256 + chip * 32
        grad_embed_ref[row : row + 32, :] = tower_ref[sender, 64:, :].astype(F32)
    send(grad_hidden_ref, grad_hidden_out)
    send(grad_embed_ref, grad_embed_out)
    grad = jnp.concatenate(
        [pieces_ref[piece].astype(F32)[:8] for piece in range(DP)], axis=0
    ).astype(BF16)
    length = first_ref.shape[0] // STEPS
    correct_one = 1.0 - BETA_ONE**ADAM_STEP
    correct_two = 1.0 - BETA_TWO**ADAM_STEP
    for step in range(STEPS):
        rows = pl.ds(step * length, length)
        place = lax.broadcasted_iota(jnp.int32, (length, BLOCK), 0) + step * length
        onehot = place == rows_ref[...]
        table_grad = dot(onehot.astype(F32).astype(BF16), grad)
        new_first = BETA_ONE * first_ref[rows, :] + (1.0 - BETA_ONE) * table_grad
        new_second = BETA_TWO * second_ref[rows, :] + (1.0 - BETA_TWO) * table_grad * table_grad
        new_first_ref[rows, :] = new_first
        new_second_ref[rows, :] = new_second
        direction_ref[rows, :] = (
            new_first / correct_one / (jnp.sqrt(new_second / correct_two) + EPSILON)
        )
        send(new_first_ref.at[rows], new_first_out.at[rows])
        send(new_second_ref.at[rows], new_second_out.at[rows])
        send(direction_ref.at[rows], direction_out.at[rows])
    for copy in copies:
        copy.wait()


def in_vmem(kernel, array, shape):
    vmem = pl.BlockSpec(memory_space=pltpu.VMEM)
    return pl.pallas_call(
        kernel,
        in_specs=[vmem],
        out_specs=vmem,
        out_shape=jax.ShapeDtypeStruct(shape, BF16),
        compiler_params=PARAMS,
    )(array)


def swap(array, axes):
    return lax.all_to_all(array, axes, 0, 0, tiled=True)


def tower_call(core, states, next_states, next_slate_t, slate_t, chosen, w_hidden, w_embed):
    sessions = states.shape[0]
    hidden, embed = w_embed.shape
    vmem = pl.BlockSpec(memory_space=pltpu.VMEM)
    places = jax.ShapeDtypeStruct((sessions, 128), jnp.int32)
    return pl.pallas_call(
        tower_kernel,
        in_specs=[pl.BlockSpec(memory_space=pltpu.SMEM)] + [vmem] * 7,
        out_specs=[vmem] * 6,
        out_shape=[
            jax.ShapeDtypeStruct((hidden, sessions), BF16),
            jax.ShapeDtypeStruct((embed, sessions), BF16),
            jax.ShapeDtypeStruct((sessions, embed), BF16),
            places,
            places,
            jax.ShapeDtypeStruct((1, sessions), jnp.int32),
        ],
        compiler_params=PARAMS,
    )(core, states, next_states, next_slate_t, slate_t, chosen, w_hidden, w_embed)


def own_call(towers, own):
    sessions = towers[1].shape[1]
    vmem = pl.BlockSpec(memory_space=pltpu.VMEM)
    line = jax.ShapeDtypeStruct((8, sessions), F32)
    return pl.pallas_call(
        own_kernel,
        in_specs=[vmem] * 6,
        out_specs=[vmem] * 4,
        out_shape=[
            jax.ShapeDtypeStruct((CHIPS, BLOCK, sessions), F32),
            line,
            line,
            jax.ShapeDtypeStruct((sessions, 128), F32),
        ],
        scratch_shapes=[pltpu.VMEM((CHIPS * 2, sessions, 128), F32)],
        compiler_params=PARAMS,
    )(*towers[1:], own)


def main_call(core, states, towers, rewards, own, other, begun, w_embed):
    sessions = states.shape[0]
    hidden, embed = w_embed.shape
    vmem = pl.BlockSpec(memory_space=pltpu.VMEM)
    scalar = pl.BlockSpec(memory_space=pltpu.SMEM)
    send, delta, *rest = pl.pallas_call(
        main_kernel,
        in_specs=[scalar] + [vmem] * 15,
        out_specs=[vmem] * 5,
        out_shape=[
            jax.ShapeDtypeStruct((CHIPS, PACK, embed), BF16),
            jax.ShapeDtypeStruct((1, sessions), F32),
            jax.ShapeDtypeStruct((CHIPS, BLOCK, sessions), BF16),
            jax.ShapeDtypeStruct((embed, sessions), BF16),
            jax.ShapeDtypeStruct((hidden, sessions), BF16),
        ],
        scratch_shapes=[
            pltpu.VMEM((CORES, CHIPS, BLOCK, sessions), F32),
            pltpu.VMEM((CHIPS * 2, sessions, 128), F32),
            pltpu.VMEM((sessions, 128), F32),
            pltpu.VMEM((CHIPS, BLOCK, sessions), BF16),
        ],
        compiler_params=PARAMS,
    )(core, states, *towers, rewards, own, other, *begun, w_embed)
    keep = pl.pallas_call(
        keep_kernel,
        in_specs=[scalar] + [vmem] * 6,
        out_specs=vmem,
        out_shape=jax.ShapeDtypeStruct((CHIPS, PACK, embed), F32),
        compiler_params=PARAMS,
    )(core, states, *towers[:2], *rest)
    return keep, send, delta


def shards(
    states,
    next_states,
    rewards,
    slate_ids,
    chosen,
    next_slate,
    table,
    first_moment,
    second_moment,
    cand_rows,
    w_hidden,
    w_embed,
):
    embed = table.shape[1]
    sessions = states.shape[0]
    vmem = pl.BlockSpec(memory_space=pltpu.VMEM)
    rows = cand_rows.reshape(1, BLOCK)
    pair = [(0, 1), (1, 0)]

    local_rows = table.at[cand_rows].get(
        mode="promise_in_bounds", unique_indices=True, wrap_negative_indices=False
    )
    copies = in_vmem(copies_kernel, local_rows, (CHIPS, BLOCK, embed))
    core = lax.axis_index("c").astype(jnp.int32).reshape(1)
    chosen = chosen.reshape(1, sessions)
    towers = tower_call(
        core, states, next_states, next_slate.T, slate_ids.T, chosen, w_hidden, w_embed
    )
    own = swap(copies, ("x", "l"))
    other = lax.ppermute(own, "c", pair)
    begun = own_call(towers, own)
    rewards = rewards.reshape(1, sessions)
    keep, send, delta = main_call(core, states, towers, rewards, own, other, begun, w_embed)

    got = lax.ppermute(send, "c", pair)
    part = (keep + got.astype(F32)).astype(BF16)
    pieces = in_vmem(cut_kernel, swap(part, ("x", "l")), (DP, PIECE, embed))
    pieces = in_vmem(piece_kernel, swap(pieces, ("z", "h")), (DP, PIECE, embed))
    pieces = swap(pieces, ("z", "h"))
    tower = in_vmem(tower_copies_kernel, pieces, (CHIPS * CORES, PACK - BLOCK, embed))
    tower = swap(tower, ("x", "c", "l"))

    last = [jax.ShapeDtypeStruct(first_moment.shape, F32)] * 3
    last += [jax.ShapeDtypeStruct(array.shape, F32) for array in (w_hidden, w_embed)]
    new_first, new_second, direction, grad_hidden, grad_embed = pl.pallas_call(
        adam_kernel,
        in_specs=[vmem] * 5,
        out_specs=[pl.BlockSpec(memory_space=pl.ANY)] * 5,
        out_shape=last,
        scratch_shapes=[pltpu.VMEM(out.shape, F32) for out in last]
        + [pltpu.SemaphoreType.DMA((2 + 3 * STEPS,))],
        compiler_params=PARAMS,
    )(rows, pieces, first_moment, second_moment, tower)
    return (new_first, new_second, direction, grad_hidden, grad_embed, delta.reshape(sessions))


def solution(mesh):
    torus = Mesh(mesh.devices.reshape(SIZES), AXES)
    every = P(AXES)
    item = P(ITEM)
    placed = (every,) * 6 + (item,) * 4 + (P(), P())
    return jax.shard_map(
        shards,
        mesh=torus,
        in_specs=placed,
        out_specs=(item, item, item, P(), P(), every),
        check_vma=False,
    )
```
